32 devices in a mesh: chan: 8 (over z, y), rep: 4 (over x, core).
Axes of the slice: x: 2, y: 2, z: 4, core: 2. Of those that a mesh axis runs over, the one named last changes fastest.
Arguments:
- records: bfloat16 [2, 8, 256, 2048], P(None, None, 'rep', 'chan'), may hold values from -6 to 6
- sources: int32 [128], replicated, may hold values from 0 to 2047
- dead_list: int32 [2, 128], replicated, may hold values from 0 to 2047
Outputs:
- correlations: float32 [128, 64, 2048], P('rep', None, 'chan')
The draws below stay inside these ranges and needn't reach their ends.
All inputs are finite; a program needn't handle non-finite values.
Results may differ from the reference program's by a relative error of at most 0.0072.
Values may be sent and summed in bfloat16 or wider, within the bound.
No kernel may reach another device: no remote copies, remote signals or barrier semaphores. Data moves between devices by JAX's collectives and lax.ppermute only.
A program may use at most 64 MiB of HBM per device.

```python
import math
import jax
import jax.numpy as jnp
from jax import lax

STACK_WINDOWS = 2
WINDOW_SAMPLES = 2048
K = 256
K0 = 16
HALF = 32
WH = 32
LAGS = 64
SRC = 128
CHANNELS_PER_BLK = 256
CH = 2048
NDEAD = 128
N_CHAN = 8
N_REP = 4


def plant(drawn, key, smallest, high):
    dims = drawn.shape
    spot = [jax.random.randint(jax.random.fold_in(key, axis), (), 0, dims[axis]) for axis in range(len(dims))]
    drawn = drawn.at[tuple(spot)].set(smallest)
    longest = dims.index(max(dims))
    spot[longest] = (spot[longest] + 1) % dims[longest]
    return drawn.at[tuple(spot)].set(high)


def shard_levels(stream_key, dims, pieces, least, high):
    loudness, own = 1.0, jax.random.fold_in(stream_key, 6)
    for dim, blocks in pieces:
        draws = jnp.exp(jax.random.uniform(jax.random.fold_in(own, dim), (blocks,), jnp.float32, least / len(pieces), high / len(pieces)))
        loudness = loudness * jnp.repeat(draws, dims[dim] // blocks).reshape([-1 if axis == dim else 1 for axis in range(len(dims))])
    return loudness


def gaussian(stream_key, extent, deviation, most, shards=(), kind=jnp.bfloat16):
    factor_of = shard_levels(stream_key, extent, shards, -0.22, 0.18) if shards else 1.0
    values = jax.random.normal(stream_key, extent, jnp.float32) * deviation * factor_of
    return jnp.minimum(jnp.maximum(values, -most), most).astype(kind)


def setup_inputs(seed: int = 0) -> dict:
    splits = jax.random.split(jax.random.key(seed), 4)
    records = gaussian(splits[0], (STACK_WINDOWS, N_CHAN, CHANNELS_PER_BLK, WINDOW_SAMPLES), 1.0, 6.0, ((2, 4), (3, 8)))
    sources = plant(jax.random.randint(splits[1], (SRC,), 0, CH), jax.random.fold_in(splits[1], 1), 0, CH - 1).astype(jnp.int32)
    dead_list = plant(jax.random.randint(splits[2], (STACK_WINDOWS, NDEAD), 0, CH), jax.random.fold_in(splits[2], 1), 0, CH - 1).astype(jnp.int32)
    return dict(records=records, sources=sources, dead_list=dead_list)


tile_span = 128
tiny_eps = 1e-06

def live_table(dead_list, total):
    window_count, listed = dead_list.shape
    window_rows = jnp.broadcast_to(jnp.arange(window_count, dtype=jnp.int32)[:, None], (window_count, listed))
    return jnp.ones((window_count, total), jnp.float32).at[window_rows, dead_list].set(0.0)

def running_mean(records):
    length = records.shape[-1]
    blocks = length // tile_span
    leading = records.shape[:-1]
    magnitude = jnp.abs(records)
    padded = jnp.pad(magnitude, [(0, 0)] * (records.ndim - 1) + [(tile_span, tile_span)])
    before = padded[..., :length].reshape(leading + (blocks, tile_span))
    middle = magnitude.reshape(leading + (blocks, tile_span))
    after = padded[..., 2 * tile_span:].reshape(leading + (blocks, tile_span))
    views = jnp.concatenate([before, middle, after], axis=-1).reshape(-1, 3 * tile_span)
    offsets = jnp.arange(3 * tile_span, dtype=jnp.int32)[:, None] - tile_span
    targets = jnp.arange(tile_span, dtype=jnp.int32)[None, :]
    band_unit_mask = (jnp.abs(offsets - targets) <= HALF).astype(jnp.bfloat16)
    totals = jnp.dot(views, band_unit_mask, preferred_element_type=jnp.float32).reshape(leading + (length,))
    sample = jnp.arange(length, dtype=jnp.int32)
    counts = (jnp.minimum(sample, HALF) + jnp.minimum(length - 1 - sample, HALF) + 1).astype(jnp.float32)
    return totals / counts

def dft_table(length):
    sample = jnp.arange(length, dtype=jnp.int32)[:, None]
    bin_index = K0 + jnp.arange(K, dtype=jnp.int32)[None, :]
    phase = sample * bin_index % length
    angle = phase.astype(jnp.float32) * (2.0 * math.pi / length)
    return jnp.concatenate([jnp.cos(angle), -jnp.sin(angle)], axis=1).astype(jnp.bfloat16)

def whiten(spectrum):
    real_part = spectrum[:, :K]
    imag_part = spectrum[:, K:]
    amplitude = jnp.sqrt(real_part * real_part + imag_part * imag_part)
    index_row = jnp.arange(K, dtype=jnp.int32)[:, None]
    index_col = jnp.arange(K, dtype=jnp.int32)[None, :]
    band = (jnp.abs(index_row - index_col) <= WH).astype(jnp.float32)
    smoothed_amplitude = jnp.dot(amplitude, band, precision=lax.Precision.HIGHEST) / lax.optimization_barrier(jnp.sum(band, axis=0))
    return (spectrum / (jnp.concatenate([smoothed_amplitude, smoothed_amplitude], axis=1) + tiny_eps)).astype(jnp.bfloat16)

def preprocess(records):
    mean_abs = running_mean(records)
    normed = (records.astype(jnp.float32) / (mean_abs + tiny_eps)).astype(jnp.bfloat16)
    spectrum = jnp.dot(normed, dft_table(records.shape[-1]), preferred_element_type=jnp.float32)
    return whiten(spectrum)

def lag_kernel(source_spectrum):
    bin_index = K0 + jnp.arange(K, dtype=jnp.int32)[None, :]
    lag_index = jnp.arange(LAGS, dtype=jnp.int32)[:, None] - LAGS // 2
    phase = jnp.mod(lag_index * bin_index, WINDOW_SAMPLES)
    angle = phase.astype(jnp.float32) * (2.0 * math.pi / WINDOW_SAMPLES)
    cosine_lookup = jnp.cos(angle)[None, :, None, :]
    sin_table = jnp.sin(angle)[None, :, None, :]
    real_part = source_spectrum[:, None, :, :K].astype(jnp.float32)
    imag_part = source_spectrum[:, None, :, K:].astype(jnp.float32)
    with_real = real_part * cosine_lookup + imag_part * sin_table
    with_imag = imag_part * cosine_lookup - real_part * sin_table
    return jnp.concatenate([with_real, with_imag], axis=3).astype(jnp.bfloat16)

def correlate(kernel, spectra_wide, source_live, chan_live):
    summed = lax.dot_general(kernel.astype(jnp.float32), spectra_wide, (((2, 3), (0, 2)), ((), ())), precision=lax.Precision.HIGHEST)
    pairs = jnp.dot(source_live.T, chan_live, precision=lax.Precision.HIGHEST)
    return summed / (math.sqrt(K) * jnp.maximum(pairs, 1.0))[:, None, :]

def reference(records, sources, dead_list):
    window_count, groups, group_share, length = records.shape
    total = groups * group_share
    live = live_table(dead_list, total)
    flat = records.reshape(window_count, total, length)
    masked = jnp.where(live[:, :, None] > 0.5, flat, jnp.zeros_like(flat))
    spectra = lax.map(preprocess, masked.reshape(-1, group_share, length)).reshape(window_count, total, 2 * K)
    source_spectrum = jnp.transpose(spectra[:, sources, :], (1, 0, 2))
    source_live = live[:, sources]
    quarter = SRC // N_REP
    spectra_wide = spectra.astype(jnp.float32)

    def one_block(block):
        return correlate(lag_kernel(block[0]), spectra_wide, block[1], live)
    blocks = (source_spectrum.reshape(N_REP, quarter, window_count, 2 * K), jnp.transpose(source_live.reshape(window_count, N_REP, quarter), (1, 0, 2)))
    result = lax.map(one_block, blocks)
    return result.reshape(SRC, LAGS, total)
```

```python
import functools
import math

import jax
import jax.numpy as jnp
import numpy as np
from jax import lax
from jax.experimental import pallas as pl
from jax.experimental.pallas import tpu as pltpu
from jax.sharding import PartitionSpec as P

WINDOW_SAMPLES = 2048
K = 256
K0 = 16
HALF = 32
WH = 32
LAGS = 64
EPS = 1e-06

CHUNK = 256
EDGE = 128
VMEM = pl.BlockSpec(memory_space=pltpu.VMEM)
LIMIT = 40 * 1024 * 1024


def dft_table(length):
    sample = np.arange(length, dtype=np.int64)[:, None]
    bin_index = K0 + np.arange(K, dtype=np.int64)[None, :]
    angle = (sample * bin_index % length) * (2.0 * math.pi / length)
    table = np.concatenate([np.cos(angle), -np.sin(angle)], axis=1)
    return table.astype(np.float32).astype(jnp.bfloat16)


def lag_tables():
    bin_index = K0 + np.arange(K, dtype=np.int64)[None, :]
    lag = np.arange(LAGS, dtype=np.int64)[:, None] - LAGS // 2
    angle = np.mod(lag * bin_index, WINDOW_SAMPLES) * (2.0 * math.pi / WINDOW_SAMPLES)
    return np.cos(angle).astype(np.float32), np.sin(angle).astype(np.float32)


def sample_band():
    source = np.arange(CHUNK + 2 * EDGE)[:, None] - EDGE
    target = np.arange(CHUNK)[None, :]
    return (np.abs(source - target) <= HALF).astype(np.float32).astype(jnp.bfloat16)


def bin_band():
    row = np.arange(K)[:, None]
    column = np.arange(K)[None, :]
    band = np.abs(row - column) <= WH
    inverse = 1.0 / band.sum(axis=0, keepdims=True)
    return band.astype(np.float32).astype(jnp.bfloat16), inverse.astype(np.float32)


def iota(shape, dim):
    return lax.broadcasted_iota(jnp.int32, shape, dim)


def pack_kernel(cw, rec_ref, src_ref, out_ref, keep_ref, give_ref, pick_ref):
    windows, groups, width, span = rec_ref.shape
    reps = cw // width
    rep = lax.axis_index("rep")
    per = groups // out_ref.shape[0]
    for w in range(windows):
        for g in range(groups):
            out_ref[g // per, w, g % per] = rec_ref[w, g]
    count = src_ref.shape[1]
    column = jnp.broadcast_to(src_ref[...], (count, count)).T
    local = groups * width
    place = iota((count, local), 1)
    ids = (place // width) * cw + rep * width + place % width
    wide = jnp.concatenate([column] * (local // count), axis=1)
    onehot = jnp.where(wide == ids, 1.0, 0.0).astype(jnp.bfloat16)
    quarter = count // reps
    for w in range(windows):
        rows = rec_ref[w].reshape(local, span)
        picked = jnp.dot(onehot, rows, preferred_element_type=jnp.float32)
        pick_ref[...] = picked
        for half in range(reps // 2):
            for ref, bit in ((keep_ref, rep % 2), (give_ref, 1 - rep % 2)):
                first = pl.multiple_of((2 * half + bit) * quarter, quarter)
                ref[half, w] = pick_ref[pl.ds(first, quarter), :].astype(jnp.bfloat16)


def pack(records, sources, chans, reps):
    windows, groups, width, span = records.shape
    count = sources.shape[0]
    part = (reps // 2, windows, count // reps, span)
    return pl.pallas_call(
        functools.partial(pack_kernel, width * reps),
        out_shape=(
            jax.ShapeDtypeStruct((chans, windows, groups // chans, width, span), jnp.bfloat16),
            jax.ShapeDtypeStruct(part, jnp.bfloat16),
            jax.ShapeDtypeStruct(part, jnp.bfloat16),
        ),
        in_specs=[VMEM, VMEM],
        out_specs=(VMEM, VMEM, VMEM),
        scratch_shapes=[pltpu.VMEM((count, span), jnp.float32)],
        compiler_params=pltpu.CompilerParams(vmem_limit_bytes=LIMIT),
        name="pack",
    )(records, sources.reshape(1, count))


def listed(ids, dead_row):
    hit = jnp.where(ids == dead_row, 1.0, 0.0)
    return jnp.max(hit, axis=1, keepdims=True)


def whiten_rows(x_ref, ext_ref, table_ref, band_ref, bins_ref, inverse_ref):
    pieces, rows, _ = x_ref.shape
    length = pieces * CHUNK
    for i in range(pieces):
        here = pl.ds(i * rows, rows)
        ext_ref[here, EDGE : EDGE + CHUNK] = jnp.abs(x_ref[i])
        blank = jnp.zeros((rows, EDGE), jnp.bfloat16)
        ext_ref[here, :EDGE] = jnp.abs(x_ref[i - 1, :, CHUNK - EDGE :]) if i else blank
        ext_ref[here, EDGE + CHUNK :] = (
            jnp.abs(x_ref[i + 1, :, :EDGE]) if i < pieces - 1 else blank
        )
    totals = jnp.dot(ext_ref[...], band_ref[...], preferred_element_type=jnp.float32)
    spectrum = jnp.zeros((rows, 2 * K), jnp.float32)
    for i in range(pieces):
        sample = iota((1, CHUNK), 1) + i * CHUNK
        counts = jnp.minimum(sample, HALF) + jnp.minimum(length - 1 - sample, HALF) + 1
        mean = totals[i * rows : (i + 1) * rows] * (1.0 / counts.astype(jnp.float32))
        normed = (x_ref[i].astype(jnp.float32) / (mean + EPS)).astype(jnp.bfloat16)
        spectrum += jnp.dot(
            normed, table_ref[i * CHUNK : (i + 1) * CHUNK, :], preferred_element_type=jnp.float32
        )
    real_part, imag_part = spectrum[:, :K], spectrum[:, K:]
    amplitude = jnp.sqrt(real_part * real_part + imag_part * imag_part)
    high = amplitude.astype(jnp.bfloat16)
    rest = amplitude - high.astype(jnp.float32)
    middle = rest.astype(jnp.bfloat16)
    low = (rest - middle.astype(jnp.float32)).astype(jnp.bfloat16)
    stacked = jnp.concatenate([high, middle, low], axis=0)
    sums = jnp.dot(stacked, bins_ref[...], preferred_element_type=jnp.float32)
    smooth = (sums[:rows] + sums[rows : 2 * rows] + sums[2 * rows :]) * inverse_ref[...]
    scale = 1.0 / (smooth + EPS)
    return real_part * scale, imag_part * scale


def channel_kernel(cw, width, x_ref, dead_ref, table_ref, band_ref, bins_ref, inverse_ref, out_ref, ext_ref):
    windows, per = out_ref.shape[0], out_ref.shape[1] // width
    real_part, imag_part = whiten_rows(x_ref, ext_ref, table_ref, band_ref, bins_ref, inverse_ref)
    block = lax.axis_index("chan") * per
    rep = lax.axis_index("rep")
    count = per * width
    row = iota((count, 1), 0)
    ids = (block + row // width) * cw + rep * width + row % width
    for w in range(windows):
        live = 1.0 - listed(ids, dead_ref[w : w + 1, :])
        here = slice(w * count, (w + 1) * count)
        out_ref[w, :, :K] = (real_part[here] * live).astype(jnp.bfloat16)
        out_ref[w, :, K:] = (imag_part[here] * live).astype(jnp.bfloat16)


def channel_spectra(x, dead_list, tables, windows, cw, width):
    pieces, rows, _ = x.shape
    return pl.pallas_call(
        functools.partial(channel_kernel, cw, width),
        out_shape=jax.ShapeDtypeStruct((windows, rows // windows, 2 * K), jnp.bfloat16),
        in_specs=[VMEM] * 6,
        out_specs=VMEM,
        scratch_shapes=[pltpu.VMEM((pieces * rows, CHUNK + 2 * EDGE), jnp.bfloat16)],
        compiler_params=pltpu.CompilerParams(vmem_limit_bytes=LIMIT),
        cost_estimate=pl.CostEstimate(
            flops=2 * rows * 2048 * 1024, bytes_accessed=4 << 20, transcendentals=0
        ),
        name="channel_spectra",
    )(x, dead_list, *tables)


def source_kernel(keys, *refs):
    parts = refs[: len(keys)]
    src_ref, dead_ref, table_ref, band_ref, bins_ref, inverse_ref, out_ref, x_ref, ext_ref = refs[len(keys) :]
    chan = lax.axis_index("chan")
    for part, slots in zip(parts, keys):
        for n, key in enumerate(slots):
            x_ref[chan ^ key if key is not None else n] = part[n]
    real_part, imag_part = whiten_rows(x_ref, ext_ref, table_ref, band_ref, bins_ref, inverse_ref)
    windows = dead_ref.shape[0]
    quarter = out_ref.shape[0] // windows
    first = pl.multiple_of(lax.axis_index("rep") * quarter, quarter)
    mine = src_ref[pl.ds(first, quarter), :]
    for w in range(windows):
        live = 1.0 - listed(mine, dead_ref[w : w + 1, :])
        here = slice(w * quarter, (w + 1) * quarter)
        out_ref[here, :K] = (real_part[here] * live).astype(jnp.bfloat16).astype(jnp.float32)
        out_ref[here, K:] = (imag_part[here] * live).astype(jnp.bfloat16).astype(jnp.float32)


def source_spectra(parts, keys, sources, dead_list, tables):
    rows = parts[0].shape[1]
    pieces = sum(len(slots) for slots in keys)
    return pl.pallas_call(
        functools.partial(source_kernel, keys),
        out_shape=jax.ShapeDtypeStruct((rows, 2 * K), jnp.float32),
        in_specs=[VMEM] * (len(parts) + 6),
        out_specs=VMEM,
        scratch_shapes=[
            pltpu.VMEM((pieces, rows, CHUNK), jnp.bfloat16),
            pltpu.VMEM((pieces * rows, CHUNK + 2 * EDGE), jnp.bfloat16),
        ],
        compiler_params=pltpu.CompilerParams(vmem_limit_bytes=LIMIT),
        cost_estimate=pl.CostEstimate(
            flops=2 * rows * 2048 * 1024, bytes_accessed=4 << 20, transcendentals=0
        ),
        name="source_spectra",
    )(*parts, sources.reshape(-1, 1), dead_list, *tables)


def correlate_kernel(flips, cw, width, *refs):
    parts = refs[: len(flips)]
    spec_ref, src_ref, dead_ref, dead_t_ref, cos_ref, sin_ref, out_ref = refs[len(flips) : -2]
    right_ref, scale_ref = refs[-2:]
    windows, _, features = parts[0].shape
    step = pl.program_id(0)
    batch, lags, columns = out_ref.shape
    per = columns // cw
    quarter = spec_ref.shape[0] // windows

    @pl.when(step == 0)
    def _():
        rep = lax.axis_index("rep")
        for part, flip in zip(parts, flips):
            for w in range(windows):
                for g in range(per):
                    first = pl.multiple_of(g * cw + (rep ^ flip) * width, width)
                    right_ref[pl.ds(first, width), pl.ds(w * features, features)] = part[
                        w, pl.ds(g * width, width), :
                    ]
        ids = lax.axis_index("chan") * columns + iota((1, columns), 1)
        pairs = jnp.zeros((quarter, columns), jnp.float32)
        mine = src_ref[pl.ds(pl.multiple_of(rep * quarter, quarter), quarter), :]
        for w in range(windows):
            dead = jnp.where(dead_t_ref[:, w : w + 1] == ids, 1.0, 0.0)
            channel_live = 1.0 - jnp.max(dead, axis=0, keepdims=True)
            source_live = 1.0 - listed(mine, dead_ref[w : w + 1, :])
            pairs += source_live * channel_live
        scale_ref[...] = 1.0 / (math.sqrt(K) * jnp.maximum(pairs, 1.0))

    left = []
    for n in range(batch):
        s = step * batch + n
        row = []
        for w in range(windows):
            bins = spec_ref[pl.ds(w * quarter + s, 1), :]
            u, v = bins[:, :K], bins[:, K:]
            row.append((u * cos_ref[...] + v * sin_ref[...]).astype(jnp.bfloat16))
            row.append((v * cos_ref[...] - u * sin_ref[...]).astype(jnp.bfloat16))
        left.append(jnp.concatenate(row, axis=1))
    summed = lax.dot_general(
        jnp.concatenate(left, axis=0),
        right_ref[...],
        (((1,), (1,)), ((), ())),
        preferred_element_type=jnp.float32,
    )
    for n in range(batch):
        out_ref[n] = summed[n * lags : (n + 1) * lags] * scale_ref[pl.ds(step * batch + n, 1), :]


def correlate(parts, flips, source_spec, sources, dead_list, cw, width, columns):
    windows = dead_list.shape[0]
    quarter = source_spec.shape[0] // windows
    batch = 4
    cosine, sine = lag_tables()

    def whole(array):
        rank = array.ndim
        return pl.BlockSpec(array.shape, lambda i: (0,) * rank)

    operands = list(parts) + [
        source_spec, sources.reshape(-1, 1), dead_list, dead_list.T, jnp.asarray(cosine), jnp.asarray(sine)
    ]
    return pl.pallas_call(
        functools.partial(correlate_kernel, flips, cw, width),
        grid=(quarter // batch,),
        out_shape=jax.ShapeDtypeStruct((quarter, LAGS, columns), jnp.float32),
        in_specs=[whole(a) for a in operands],
        out_specs=pl.BlockSpec((batch, LAGS, columns), lambda i: (i, 0, 0)),
        scratch_shapes=[
            pltpu.VMEM((columns, windows * 2 * K), jnp.bfloat16),
            pltpu.VMEM((quarter, columns), jnp.float32),
        ],
        compiler_params=pltpu.CompilerParams(vmem_limit_bytes=LIMIT),
        name="correlate",
    )(*operands)


def swap(x, axis, flip):
    size = lax.axis_size(axis)
    return lax.ppermute(x, axis, [(i, i ^ flip) for i in range(size)])


def regroup(x):
    shards_in, rows, span = x.shape
    if span == CHUNK:
        return x
    joined = jnp.transpose(x, (1, 0, 2)).reshape(rows, -1, CHUNK)
    return jnp.transpose(joined, (1, 0, 2))


def gather_sources(keep, give):
    reps, chans = lax.axis_size("rep"), lax.axis_size("chan")
    rep, chan = lax.axis_index("rep"), lax.axis_index("chan")
    _, windows, quarter, span = keep.shape
    mine = keep + swap(give, "rep", 1)
    flip = 2
    while flip < reps:
        pairs = mine.reshape((-1, 2) + mine.shape[1:])
        bit = (rep // flip) % 2
        kept = lax.dynamic_index_in_dim(pairs, bit, 1, keepdims=False)
        given = lax.dynamic_index_in_dim(pairs, 1 - bit, 1, keepdims=False)
        mine = kept + swap(given, "rep", flip)
        flip *= 2
    held = mine.reshape(1, windows * quarter, span)
    keys = [0]
    flip = chans // 2
    while flip > 1:
        held = jnp.concatenate([held, swap(held, "chan", flip)], axis=0)
        keys = keys + [key ^ flip for key in keys]
        flip //= 2
    other = swap(held, "chan", 1)
    if span == CHUNK:
        return (held, other), (tuple(keys), tuple(key ^ 1 for key in keys))
    every = jnp.concatenate([held, other], axis=0)
    keys = jnp.asarray(keys + [key ^ 1 for key in keys], jnp.int32)
    every = jnp.zeros_like(every).at[chan ^ keys].set(every)
    every = regroup(every)
    return (every,), ((None,) * every.shape[0],)


def shards(records, sources, dead_list):
    windows, groups, width, span = records.shape
    reps, chans = lax.axis_size("rep"), lax.axis_size("chan")
    cw = width * reps
    per = groups // chans
    blocks, keep, give = pack(records, sources, chans, reps)
    blocks = blocks.reshape(chans, windows * per * width, span)
    bins, inverse = bin_band()
    tables = [
        jnp.asarray(a) for a in (dft_table(chans * span), sample_band(), bins, inverse)
    ]
    arrived = regroup(lax.all_to_all(blocks, "chan", 0, 0, tiled=True))
    parts, keys = gather_sources(keep, give)
    spectra = channel_spectra(arrived, dead_list, tables, windows, cw, width)
    source_spec = source_spectra(parts, keys, sources, dead_list, tables)
    pieces, flips = [spectra], [0]
    flip = reps // 2
    while flip:
        pieces = pieces + [swap(piece, "rep", flip) for piece in pieces]
        flips = flips + [f ^ flip for f in flips]
        flip //= 2
    return correlate(pieces, flips, source_spec, sources, dead_list, cw, width, per * cw)


def solution(mesh):
    placed = (P(None, None, "rep", "chan"), P(), P())
    return jax.shard_map(
        shards, mesh=mesh, in_specs=placed, out_specs=P("rep", None, "chan"), check_vma=False
    )
```

```python
import functools
import math

import jax
import jax.numpy as jnp
import numpy as np
from jax import lax
from jax.experimental import pallas as pl
from jax.experimental.pallas import tpu as pltpu
from jax.sharding import PartitionSpec as P

WINDOW_SAMPLES = 2048
K = 256
K0 = 16
HALF = 32
WH = 32
LAGS = 64
EPS = 1e-06

CHUNK = 256
EDGE = 128
VMEM = pl.BlockSpec(memory_space=pltpu.VMEM)
LIMIT = 40 * 1024 * 1024


def dft_table(length):
    sample = np.arange(length, dtype=np.int64)[:, None]
    bin_index = K0 + np.arange(K, dtype=np.int64)[None, :]
    angle = (sample * bin_index % length) * (2.0 * math.pi / length)
    table = np.concatenate([np.cos(angle), -np.sin(angle)], axis=1)
    return table.astype(np.float32).astype(jnp.bfloat16)


def lag_tables():
    bin_index = K0 + np.arange(K, dtype=np.int64)[None, :]
    lag = np.arange(LAGS, dtype=np.int64)[:, None] - LAGS // 2
    angle = np.mod(lag * bin_index, WINDOW_SAMPLES) * (2.0 * math.pi / WINDOW_SAMPLES)
    return np.cos(angle).astype(np.float32), np.sin(angle).astype(np.float32)


def sample_band():
    source = np.arange(CHUNK + 2 * EDGE)[:, None] - EDGE
    target = np.arange(CHUNK)[None, :]
    return (np.abs(source - target) <= HALF).astype(np.float32).astype(jnp.bfloat16)


def bin_band():
    row = np.arange(K)[:, None]
    column = np.arange(K)[None, :]
    band = np.abs(row - column) <= WH
    inverse = 1.0 / band.sum(axis=0, keepdims=True)
    return band.astype(np.float32).astype(jnp.bfloat16), inverse.astype(np.float32)


def iota(shape, dim):
    return lax.broadcasted_iota(jnp.int32, shape, dim)


def columns_of(row):
    return jnp.concatenate(
        [
            jnp.broadcast_to(row[:, i : i + 128], (128, 128)).T
            for i in range(0, row.shape[1], 128)
        ],
        axis=0,
    )


def listed(ids, dead):
    hit = jnp.zeros((ids.shape[0], 128), jnp.float32)
    for i in range(0, dead.shape[1], 128):
        hit = jnp.maximum(hit, jnp.where(ids == dead[:, i : i + 128], 1.0, 0.0))
    return jnp.max(hit, axis=1, keepdims=True)


def pack_kernel(
    cw, rec_hbm, src_hbm, dead_hbm,
    out_ref, keep_ref, give_ref, live_ref, source_live_ref, scale_ref,
    rec_ref, src_ref, dead_ref, pick_ref, sem,
):
    copies = [
        pltpu.make_async_copy(src_hbm, src_ref, sem.at[0]),
        pltpu.make_async_copy(dead_hbm, dead_ref, sem.at[1]),
        pltpu.make_async_copy(rec_hbm, rec_ref, sem.at[2]),
    ]
    for copy in copies:
        copy.start()
    windows, groups, width, span = rec_ref.shape
    reps = cw // width
    rep, chan = lax.axis_index("rep"), lax.axis_index("chan")
    per = groups // out_ref.shape[0]
    count = src_ref.shape[1]
    quarter = count // reps
    here = pl.ds(pl.multiple_of(rep * quarter, quarter), quarter)
    copies[0].wait()
    column = columns_of(src_ref[...])
    local = groups * width
    place = iota((count, local), 1)
    ids = (place // width) * cw + rep * width + place % width
    wide = jnp.concatenate([column] * (local // 128), axis=1)
    onehot = jnp.where(wide == ids, 1.0, 0.0).astype(jnp.bfloat16)
    copies[1].wait()
    row = iota((per * width, 1), 0)
    row_ids = (chan * per + row // width) * cw + rep * width + row % width
    block_ids = chan * per * cw + iota((1, per * cw), 1)
    pairs = jnp.zeros((count, per * cw), jnp.float32)
    for w in range(windows):
        dead = dead_ref[w : w + 1, :]
        live_ref[w * per * width : (w + 1) * per * width, :] = 1.0 - listed(row_ids, dead)
        source_live = 1.0 - listed(column, dead)
        pick_ref[:, :1] = source_live
        source_live_ref[w * quarter : (w + 1) * quarter, :] = pick_ref[here, :1]
        dead_column = columns_of(dead)
        hits = [
            jnp.max(
                jnp.where(dead_column == block_ids[:, i : i + 128], 1.0, 0.0), axis=0, keepdims=True
            )
            for i in range(0, per * cw, 128)
        ]
        pairs += source_live * (1.0 - jnp.concatenate(hits, axis=1))
    for i in range(0, per * cw, span):
        pick_ref[:, : min(span, per * cw)] = pairs[:, i : i + span]
        scale_ref[:, i : i + span] = 1.0 / (
            math.sqrt(K) * jnp.maximum(pick_ref[here, : min(span, per * cw)], 1.0)
        )
    copies[2].wait()
    for w in range(windows):
        for g in range(groups):
            out_ref[g // per, w, g % per] = rec_ref[w, g]
    for w in range(windows):
        rows = rec_ref[w].reshape(local, span)
        pick_ref[...] = jnp.dot(onehot, rows, preferred_element_type=jnp.float32)
        for half in range(reps // 2):
            for ref, bit in ((keep_ref, rep % 2), (give_ref, 1 - rep % 2)):
                first = pl.multiple_of((2 * half + bit) * quarter, quarter)
                ref[half, w] = pick_ref[pl.ds(first, quarter), :].astype(jnp.bfloat16)


def pack(records, sources, dead_list, chans, reps):
    windows, groups, width, span = records.shape
    count = sources.shape[0]
    per = groups // chans
    part = (reps // 2, windows, count // reps, span)
    anywhere = pl.BlockSpec(memory_space=pl.ANY)
    return pl.pallas_call(
        functools.partial(pack_kernel, width * reps),
        out_shape=(
            jax.ShapeDtypeStruct((chans, windows, per, width, span), jnp.bfloat16),
            jax.ShapeDtypeStruct(part, jnp.bfloat16),
            jax.ShapeDtypeStruct(part, jnp.bfloat16),
            jax.ShapeDtypeStruct((windows * per * width, 1), jnp.float32),
            jax.ShapeDtypeStruct((windows * count // reps, 1), jnp.float32),
            jax.ShapeDtypeStruct((count // reps, per * width * reps), jnp.float32),
        ),
        in_specs=[anywhere] * 3,
        out_specs=(VMEM,) * 6,
        scratch_shapes=[
            pltpu.VMEM(records.shape, jnp.bfloat16),
            pltpu.VMEM((1, count), jnp.int32),
            pltpu.VMEM(dead_list.shape, jnp.int32),
            pltpu.VMEM((count, span), jnp.float32),
            pltpu.SemaphoreType.DMA((3,)),
        ],
        compiler_params=pltpu.CompilerParams(vmem_limit_bytes=LIMIT),
        name="pack",
    )(records, sources.reshape(1, count), dead_list)


def whiten_rows(x_ref, ext_ref, table_ref, band_ref, bins_ref, inverse_ref):
    pieces, rows, _ = x_ref.shape
    length = pieces * CHUNK
    for i in range(pieces):
        here = pl.ds(i * rows, rows)
        ext_ref[here, EDGE : EDGE + CHUNK] = jnp.abs(x_ref[i])
        blank = jnp.zeros((rows, EDGE), jnp.bfloat16)
        ext_ref[here, :EDGE] = jnp.abs(x_ref[i - 1, :, CHUNK - EDGE :]) if i else blank
        ext_ref[here, EDGE + CHUNK :] = (
            jnp.abs(x_ref[i + 1, :, :EDGE]) if i < pieces - 1 else blank
        )
    totals = jnp.dot(ext_ref[...], band_ref[...], preferred_element_type=jnp.float32)
    spectrum = jnp.zeros((rows, 2 * K), jnp.float32)
    for i in range(pieces):
        sample = iota((1, CHUNK), 1) + i * CHUNK
        counts = jnp.minimum(sample, HALF) + jnp.minimum(length - 1 - sample, HALF) + 1
        mean = totals[i * rows : (i + 1) * rows] * (1.0 / counts.astype(jnp.float32))
        normed = (x_ref[i].astype(jnp.float32) / (mean + EPS)).astype(jnp.bfloat16)
        spectrum += jnp.dot(
            normed, table_ref[i * CHUNK : (i + 1) * CHUNK, :], preferred_element_type=jnp.float32
        )
    real_part, imag_part = spectrum[:, :K], spectrum[:, K:]
    amplitude = jnp.sqrt(real_part * real_part + imag_part * imag_part)
    high = amplitude.astype(jnp.bfloat16)
    rest = amplitude - high.astype(jnp.float32)
    middle = rest.astype(jnp.bfloat16)
    low = (rest - middle.astype(jnp.float32)).astype(jnp.bfloat16)
    stacked = jnp.concatenate([high, middle, low], axis=0)
    sums = jnp.dot(stacked, bins_ref[...], preferred_element_type=jnp.float32)
    smooth = (sums[:rows] + sums[rows : 2 * rows] + sums[2 * rows :]) * inverse_ref[...]
    scale = 1.0 / (smooth + EPS)
    return real_part * scale, imag_part * scale


def channel_kernel(x_ref, live_ref, table_ref, band_ref, bins_ref, inverse_ref, out_ref, ext_ref):
    windows, count, _ = out_ref.shape
    real_part, imag_part = whiten_rows(x_ref, ext_ref, table_ref, band_ref, bins_ref, inverse_ref)
    for w in range(windows):
        here = slice(w * count, (w + 1) * count)
        out_ref[w, :, :K] = (real_part[here] * live_ref[here, :]).astype(jnp.bfloat16)
        out_ref[w, :, K:] = (imag_part[here] * live_ref[here, :]).astype(jnp.bfloat16)


def channel_spectra(x, live, tables, windows):
    pieces, rows, _ = x.shape
    return pl.pallas_call(
        channel_kernel,
        out_shape=jax.ShapeDtypeStruct((windows, rows // windows, 2 * K), jnp.bfloat16),
        in_specs=[VMEM] * 6,
        out_specs=VMEM,
        scratch_shapes=[pltpu.VMEM((pieces * rows, CHUNK + 2 * EDGE), jnp.bfloat16)],
        compiler_params=pltpu.CompilerParams(vmem_limit_bytes=LIMIT),
        cost_estimate=pl.CostEstimate(
            flops=2 * rows * 2048 * 1024, bytes_accessed=4 << 20, transcendentals=0
        ),
        name="channel_spectra",
    )(x, live, *tables)


def source_kernel(keys, windows, *refs):
    parts = refs[: len(keys)]
    live_ref, cos_ref, sin_ref, table_ref, band_ref, bins_ref, inverse_ref = refs[len(keys) : -3]
    out_ref, x_ref, ext_ref = refs[-3:]
    chan = lax.axis_index("chan")
    for part, slots in zip(parts, keys):
        for n, key in enumerate(slots):
            x_ref[chan ^ key if key is not None else n] = part[n]
    real_part, imag_part = whiten_rows(x_ref, ext_ref, table_ref, band_ref, bins_ref, inverse_ref)
    real_part = (real_part * live_ref[...]).astype(jnp.bfloat16).astype(jnp.float32)
    imag_part = (imag_part * live_ref[...]).astype(jnp.bfloat16).astype(jnp.float32)
    quarter = real_part.shape[0] // windows
    lags = cos_ref.shape[0]
    for s in range(quarter):
        for w in range(windows):
            u = real_part[w * quarter + s : w * quarter + s + 1, :]
            v = imag_part[w * quarter + s : w * quarter + s + 1, :]
            rows = slice(s * lags, (s + 1) * lags)
            first = w * 2 * K
            out_ref[rows, first : first + K] = (
                u * cos_ref[...] + v * sin_ref[...]
            ).astype(jnp.bfloat16)
            out_ref[rows, first + K : first + 2 * K] = (
                v * cos_ref[...] - u * sin_ref[...]
            ).astype(jnp.bfloat16)


def source_kernels(parts, keys, live, tables, windows):
    rows = parts[0].shape[1]
    pieces = sum(len(slots) for slots in keys)
    cosine, sine = lag_tables()
    return pl.pallas_call(
        functools.partial(source_kernel, keys, windows),
        out_shape=jax.ShapeDtypeStruct((rows // windows * LAGS, windows * 2 * K), jnp.bfloat16),
        in_specs=[VMEM] * (len(parts) + 7),
        out_specs=VMEM,
        scratch_shapes=[
            pltpu.VMEM((pieces, rows, CHUNK), jnp.bfloat16),
            pltpu.VMEM((pieces * rows, CHUNK + 2 * EDGE), jnp.bfloat16),
        ],
        compiler_params=pltpu.CompilerParams(vmem_limit_bytes=LIMIT),
        cost_estimate=pl.CostEstimate(
            flops=2 * rows * 2048 * 1024, bytes_accessed=8 << 20, transcendentals=0
        ),
        name="source_kernels",
    )(*parts, live, jnp.asarray(cosine), jnp.asarray(sine), *tables)


def correlate_kernel(flips, cw, *refs):
    parts = refs[: len(flips)]
    left_ref, scale_ref, out_ref, right_ref = refs[len(flips) :]
    windows, count, features = parts[0].shape
    batch, lags, columns = out_ref.shape
    per = columns // cw
    width = count // per

    @pl.when(pl.program_id(0) == 0)
    def _():
        rep = lax.axis_index("rep")
        for part, flip in zip(parts, flips):
            for w in range(windows):
                for g in range(per):
                    first = pl.multiple_of(g * cw + (rep ^ flip) * width, width)
                    right_ref[pl.ds(first, width), pl.ds(w * features, features)] = part[
                        w, pl.ds(g * width, width), :
                    ]

    summed = lax.dot_general(
        left_ref[...], right_ref[...], (((1,), (1,)), ((), ())), preferred_element_type=jnp.float32
    )
    for n in range(batch):
        scale = scale_ref[pl.ds(pl.program_id(0) * batch + n, 1), :]
        out_ref[n] = summed[n * lags : (n + 1) * lags] * scale


def correlate(parts, flips, left, scale, cw):
    quarter, columns = scale.shape
    batch = 8

    def whole(array):
        rank = array.ndim
        return pl.BlockSpec(array.shape, lambda i: (0,) * rank)

    return pl.pallas_call(
        functools.partial(correlate_kernel, flips, cw),
        grid=(quarter // batch,),
        out_shape=jax.ShapeDtypeStruct((quarter, LAGS, columns), jnp.float32),
        in_specs=[whole(part) for part in parts]
        + [pl.BlockSpec((batch * LAGS, left.shape[1]), lambda i: (i, 0)), whole(scale)],
        out_specs=pl.BlockSpec((batch, LAGS, columns), lambda i: (i, 0, 0)),
        scratch_shapes=[pltpu.VMEM((columns, left.shape[1]), jnp.bfloat16)],
        compiler_params=pltpu.CompilerParams(vmem_limit_bytes=LIMIT),
        name="correlate",
    )(*parts, left, scale)


def swap(x, axis, flip):
    size = lax.axis_size(axis)
    return lax.ppermute(x, axis, [(i, i ^ flip) for i in range(size)])


def regroup(x):
    shards_in, rows, span = x.shape
    if span == CHUNK:
        return x
    joined = jnp.transpose(x, (1, 0, 2)).reshape(rows, -1, CHUNK)
    return jnp.transpose(joined, (1, 0, 2))


def gather_sources(keep, give):
    reps, chans = lax.axis_size("rep"), lax.axis_size("chan")
    rep, chan = lax.axis_index("rep"), lax.axis_index("chan")
    _, windows, quarter, span = keep.shape
    mine = keep + swap(give, "rep", 1)
    flip = 2
    while flip < reps:
        pairs = mine.reshape((-1, 2) + mine.shape[1:])
        bit = (rep // flip) % 2
        kept = lax.dynamic_index_in_dim(pairs, bit, 1, keepdims=False)
        given = lax.dynamic_index_in_dim(pairs, 1 - bit, 1, keepdims=False)
        mine = kept + swap(given, "rep", flip)
        flip *= 2
    held = mine.reshape(1, windows * quarter, span)
    near = min(4, chans // 2)
    keys = list(range(near))
    held = jnp.concatenate([held] + [swap(held, "chan", key) for key in keys[1:]], axis=0)
    flip = near
    while flip < chans // 2:
        held = jnp.concatenate([held, swap(held, "chan", flip)], axis=0)
        keys = keys + [key ^ flip for key in keys]
        flip *= 2
    other = swap(held, "chan", flip)
    if span == CHUNK:
        return (held, other), (tuple(keys), tuple(key ^ flip for key in keys))
    every = jnp.concatenate([held, other], axis=0)
    keys = jnp.asarray(keys + [key ^ flip for key in keys], jnp.int32)
    every = jnp.zeros_like(every).at[chan ^ keys].set(every)
    every = regroup(every)
    return (every,), ((None,) * every.shape[0],)


def shards(records, sources, dead_list):
    windows, groups, width, span = records.shape
    reps, chans = lax.axis_size("rep"), lax.axis_size("chan")
    cw = width * reps
    per = groups // chans
    blocks, keep, give, live, source_live, scale = pack(records, sources, dead_list, chans, reps)
    blocks = blocks.reshape(chans, windows * per * width, span)
    bins, inverse = bin_band()
    tables = [
        jnp.asarray(a) for a in (dft_table(chans * span), sample_band(), bins, inverse)
    ]
    arrived = regroup(lax.all_to_all(blocks, "chan", 0, 0, tiled=True))
    parts, keys = gather_sources(keep, give)
    spectra = channel_spectra(arrived, live, tables, windows)
    left = source_kernels(parts, keys, source_live, tables, windows)
    pieces, flips = [spectra], [0]
    flip = reps // 2
    while flip:
        pieces = pieces + [swap(piece, "rep", flip) for piece in pieces]
        flips = flips + [f ^ flip for f in flips]
        flip //= 2
    return correlate(pieces, flips, left, scale, cw)


def solution(mesh):
    placed = (P(None, None, "rep", "chan"), P(), P())
    return jax.shard_map(
        shards, mesh=mesh, in_specs=placed, out_specs=P("rep", None, "chan"), check_vma=False
    )
```

```python
import functools
import math

import jax
import jax.numpy as jnp
import numpy as np
from jax import lax
from jax.experimental import pallas as pl
from jax.experimental.pallas import tpu as pltpu
from jax.sharding import PartitionSpec as P

WINDOW_SAMPLES = 2048
K = 256
K0 = 16
HALF = 32
WH = 32
LAGS = 64
EPS = 1e-06

CHUNK = 256
EDGE = 128
VMEM = pl.BlockSpec(memory_space=pltpu.VMEM)
LIMIT = 16 * 1024 * 1024
WHOLE = 60 * 1024 * 1024
HBM = pl.BlockSpec(memory_space=pltpu.HBM)


def dft_table(length):
    sample = np.arange(length, dtype=np.int64)[:, None]
    bin_index = K0 + np.arange(K, dtype=np.int64)[None, :]
    angle = (sample * bin_index % length) * (2.0 * math.pi / length)
    table = np.concatenate([np.cos(angle), -np.sin(angle)], axis=1)
    return table.astype(np.float32).astype(jnp.bfloat16)


def lag_tables():
    bin_index = K0 + np.arange(K, dtype=np.int64)[None, :]
    lag = np.arange(LAGS, dtype=np.int64)[:, None] - LAGS // 2
    angle = np.mod(lag * bin_index, WINDOW_SAMPLES) * (2.0 * math.pi / WINDOW_SAMPLES)
    return np.cos(angle).astype(np.float32), np.sin(angle).astype(np.float32)


def sample_band():
    source = np.arange(CHUNK + 2 * EDGE)[:, None] - EDGE
    target = np.arange(CHUNK)[None, :]
    return (np.abs(source - target) <= HALF).astype(np.float32).astype(jnp.bfloat16)


def bin_band():
    row = np.arange(K)[:, None]
    column = np.arange(K)[None, :]
    return (np.abs(row - column) <= WH).astype(np.float32).astype(jnp.bfloat16)


def iota(shape, dim):
    return lax.broadcasted_iota(jnp.int32, shape, dim)


def columns_of(row):
    return jnp.concatenate(
        [
            jnp.broadcast_to(row[:, i : i + 128], (128, 128)).T
            for i in range(0, row.shape[1], 128)
        ],
        axis=0,
    )


def listed(ids, dead):
    hit = jnp.zeros((ids.shape[0], 128), jnp.float32)
    for i in range(0, dead.shape[1], 128):
        hit = jnp.maximum(hit, jnp.where(ids == dead[:, i : i + 128], 1.0, 0.0))
    return jnp.max(hit, axis=1, keepdims=True)


def pack_kernel(
    cw, rec_hbm, src_hbm, dead_hbm,
    out_ref, *refs,
):
    part_refs = refs[:-8]
    live_ref, source_live_ref, scale_ref, rec_ref, src_ref, dead_ref, pick_ref, sem = refs[-8:]
    copies = [
        pltpu.make_async_copy(src_hbm, src_ref, sem.at[0]),
        pltpu.make_async_copy(dead_hbm, dead_ref, sem.at[1]),
        pltpu.make_async_copy(rec_hbm, rec_ref, sem.at[2]),
    ]
    for copy in copies:
        copy.start()
    windows, groups, width, span = rec_ref.shape
    per = groups // out_ref.shape[0]
    reps = cw // width
    rep, chan = lax.axis_index("rep"), lax.axis_index("chan")
    count = src_ref.shape[1]
    quarter = count // reps
    here = pl.ds(pl.multiple_of(rep * quarter, quarter), quarter)
    copies[0].wait()
    column = columns_of(src_ref[...])
    local = groups * width
    place = iota((count, local), 1)
    ids = (place // width) * cw + rep * width + place % width
    wide = jnp.concatenate([column] * (local // 128), axis=1)
    onehot = jnp.where(wide == ids, 1.0, 0.0).astype(jnp.bfloat16)
    copies[1].wait()
    row = iota((per * width, 1), 0)
    row_ids = (chan * per + row // width) * cw + rep * width + row % width
    block_ids = chan * per * cw + iota((1, per * cw), 1)
    pairs = jnp.zeros((count, per * cw), jnp.float32)
    for w in range(windows):
        dead = dead_ref[w : w + 1, :]
        live_ref[w * per * width : (w + 1) * per * width, :] = 1.0 - listed(row_ids, dead)
        source_live = 1.0 - listed(column, dead)
        pick_ref[:, :1] = source_live
        source_live_ref[w * quarter : (w + 1) * quarter, :] = pick_ref[here, :1]
        dead_column = columns_of(dead)
        hits = [
            jnp.max(
                jnp.where(dead_column == block_ids[:, i : i + 128], 1.0, 0.0), axis=0, keepdims=True
            )
            for i in range(0, per * cw, 128)
        ]
        pairs += source_live * (1.0 - jnp.concatenate(hits, axis=1))
    for i in range(0, per * cw, span):
        pick_ref[:, : min(span, per * cw)] = pairs[:, i : i + span]
        scale_ref[:, i : i + span] = 1.0 / (
            math.sqrt(K) * jnp.maximum(pick_ref[here, : min(span, per * cw)], 1.0)
        )
    copies[2].wait()
    for w in range(windows):
        for g in range(groups):
            out_ref[g // per, w, g % per] = rec_ref[w, g]
    for w in range(windows):
        rows = rec_ref[w].reshape(local, span)
        pick_ref[...] = jnp.dot(onehot, rows, preferred_element_type=jnp.float32)
        for flip, ref in enumerate(part_refs):
            first = pl.multiple_of((rep ^ flip) * quarter, quarter)
            ref[w] = pick_ref[pl.ds(first, quarter), :].astype(jnp.bfloat16)


def pack(records, sources, dead_list, chans, reps):
    windows, groups, width, span = records.shape
    count = sources.shape[0]
    per = groups // chans
    part = jax.ShapeDtypeStruct((windows, count // reps, span), jnp.bfloat16)
    return pl.pallas_call(
        functools.partial(pack_kernel, width * reps),
        out_shape=(
            jax.ShapeDtypeStruct((chans, windows, per, width, span), jnp.bfloat16),
            *[part] * reps,
            jax.ShapeDtypeStruct((windows * per * width, 1), jnp.float32),
            jax.ShapeDtypeStruct((windows * count // reps, 1), jnp.float32),
            jax.ShapeDtypeStruct((count // reps, per * width * reps), jnp.float32),
        ),
        in_specs=[HBM] * 3,
        out_specs=(VMEM,) * (reps + 4),
        scratch_shapes=[
            pltpu.VMEM(records.shape, jnp.bfloat16),
            pltpu.VMEM((1, count), jnp.int32),
            pltpu.VMEM(dead_list.shape, jnp.int32),
            pltpu.VMEM((count, span), jnp.float32),
            pltpu.SemaphoreType.DMA((3,)),
        ],
        compiler_params=pltpu.CompilerParams(vmem_limit_bytes=WHOLE),
        name="pack",
    )(records, sources.reshape(1, count), dead_list)


def whiten_rows(x_ref, ext_ref, table_ref, band_ref, bins_ref):
    pieces, rows, _ = x_ref.shape
    length = pieces * CHUNK
    for i in range(pieces):
        here = pl.ds(i * rows, rows)
        ext_ref[here, EDGE : EDGE + CHUNK] = jnp.abs(x_ref[i])
        blank = jnp.zeros((rows, EDGE), jnp.bfloat16)
        ext_ref[here, :EDGE] = jnp.abs(x_ref[i - 1, :, CHUNK - EDGE :]) if i else blank
        ext_ref[here, EDGE + CHUNK :] = (
            jnp.abs(x_ref[i + 1, :, :EDGE]) if i < pieces - 1 else blank
        )
    totals = jnp.dot(ext_ref[...], band_ref[...], preferred_element_type=jnp.float32)
    spectrum = jnp.zeros((rows, 2 * K), jnp.float32)
    for i in range(pieces):
        sample = iota((1, CHUNK), 1) + i * CHUNK
        counts = jnp.minimum(sample, HALF) + jnp.minimum(length - 1 - sample, HALF) + 1
        mean = totals[i * rows : (i + 1) * rows] * (1.0 / counts.astype(jnp.float32))
        normed = (x_ref[i].astype(jnp.float32) / (mean + EPS)).astype(jnp.bfloat16)
        spectrum += jnp.dot(
            normed, table_ref[i * CHUNK : (i + 1) * CHUNK, :], preferred_element_type=jnp.float32
        )
    real_part, imag_part = spectrum[:, :K], spectrum[:, K:]
    amplitude = jnp.sqrt(real_part * real_part + imag_part * imag_part)
    high = amplitude.astype(jnp.bfloat16)
    rest = amplitude - high.astype(jnp.float32)
    middle = rest.astype(jnp.bfloat16)
    low = (rest - middle.astype(jnp.float32)).astype(jnp.bfloat16)
    stacked = jnp.concatenate([high, middle, low], axis=0)
    sums = jnp.dot(stacked, bins_ref[...], preferred_element_type=jnp.float32)
    place = iota((1, K), 1)
    width = jnp.minimum(place, WH) + jnp.minimum(K - 1 - place, WH) + 1
    smooth = (sums[:rows] + sums[rows : 2 * rows] + sums[2 * rows :]) * (
        1.0 / width.astype(jnp.float32)
    )
    scale = 1.0 / (smooth + EPS)
    return real_part * scale, imag_part * scale


def channel_kernel(x_ref, live_ref, table_ref, band_ref, bins_ref, out_ref, ext_ref):
    windows, count, _ = out_ref.shape
    real_part, imag_part = whiten_rows(x_ref, ext_ref, table_ref, band_ref, bins_ref)
    for w in range(windows):
        here = slice(w * count, (w + 1) * count)
        out_ref[w, :, :K] = (real_part[here] * live_ref[here, :]).astype(jnp.bfloat16)
        out_ref[w, :, K:] = (imag_part[here] * live_ref[here, :]).astype(jnp.bfloat16)


def channel_spectra(x, live, tables, windows):
    pieces, rows, _ = x.shape
    return pl.pallas_call(
        channel_kernel,
        out_shape=jax.ShapeDtypeStruct((windows, rows // windows, 2 * K), jnp.bfloat16),
        in_specs=[VMEM] * 5,
        out_specs=VMEM,
        scratch_shapes=[pltpu.VMEM((pieces * rows, CHUNK + 2 * EDGE), jnp.bfloat16)],
        compiler_params=pltpu.CompilerParams(vmem_limit_bytes=LIMIT),
        cost_estimate=pl.CostEstimate(
            flops=1, bytes_accessed=1, transcendentals=0
        ),
        name="channel_spectra",
    )(x, live, *tables)


def source_kernel(keys, windows, *refs):
    parts = refs[: len(keys)]
    live_ref, cos_ref, sin_ref, table_ref, band_ref, bins_ref = refs[len(keys) : -3]
    out_ref, x_ref, ext_ref = refs[-3:]
    chan = lax.axis_index("chan")
    for part, slots in zip(parts, keys):
        for n, key in enumerate(slots):
            x_ref[chan ^ key if key is not None else n] = part[n]
    real_part, imag_part = whiten_rows(x_ref, ext_ref, table_ref, band_ref, bins_ref)
    real_part = (real_part * live_ref[...]).astype(jnp.bfloat16).astype(jnp.float32)
    imag_part = (imag_part * live_ref[...]).astype(jnp.bfloat16).astype(jnp.float32)
    quarter = real_part.shape[0] // windows
    lags = cos_ref.shape[0]
    for s in range(quarter):
        for w in range(windows):
            u = real_part[w * quarter + s : w * quarter + s + 1, :]
            v = imag_part[w * quarter + s : w * quarter + s + 1, :]
            rows = slice(s * lags, (s + 1) * lags)
            first = w * 2 * K
            out_ref[rows, first : first + K] = (
                u * cos_ref[...] + v * sin_ref[...]
            ).astype(jnp.bfloat16)
            out_ref[rows, first + K : first + 2 * K] = (
                v * cos_ref[...] - u * sin_ref[...]
            ).astype(jnp.bfloat16)


def source_kernels(parts, keys, live, tables, windows):
    rows = parts[0].shape[1]
    pieces = sum(len(slots) for slots in keys)
    cosine, sine = lag_tables()
    return pl.pallas_call(
        functools.partial(source_kernel, keys, windows),
        out_shape=jax.ShapeDtypeStruct((rows // windows * LAGS, windows * 2 * K), jnp.bfloat16),
        in_specs=[VMEM] * (len(parts) + 6),
        out_specs=VMEM,
        scratch_shapes=[
            pltpu.VMEM((pieces, rows, CHUNK), jnp.bfloat16),
            pltpu.VMEM((pieces * rows, CHUNK + 2 * EDGE), jnp.bfloat16),
        ],
        compiler_params=pltpu.CompilerParams(vmem_limit_bytes=LIMIT),
        cost_estimate=pl.CostEstimate(
            flops=1 << 34, bytes_accessed=8 << 20, transcendentals=0
        ),
        name="source_kernels",
    )(*parts, live, jnp.asarray(cosine), jnp.asarray(sine), *tables)


def correlate_kernel(flips, cw, *refs):
    parts = refs[: len(flips)]
    left_ref, scale_ref, out_hbm, right_ref, out_ref, sem = refs[len(flips) :]
    windows, count, features = parts[0].shape
    steps, batch, lags, columns = out_ref.shape
    per = columns // cw
    width = count // per
    rep = lax.axis_index("rep")
    for part, flip in zip(parts, flips):
        for w in range(windows):
            for g in range(per):
                first = pl.multiple_of(g * cw + (rep ^ flip) * width, width)
                right_ref[pl.ds(first, width), pl.ds(w * features, features)] = part[
                    w, pl.ds(g * width, width), :
                ]
    copies = []
    for i in range(steps):
        summed = lax.dot_general(
            left_ref[i * batch * lags : (i + 1) * batch * lags, :],
            right_ref[...],
            (((1,), (1,)), ((), ())),
            preferred_element_type=jnp.float32,
        )
        for n in range(batch):
            s = i * batch + n
            out_ref[i, n] = summed[n * lags : (n + 1) * lags] * scale_ref[s : s + 1, :]
        copies.append(
            pltpu.make_async_copy(
                out_ref.at[i], out_hbm.at[pl.ds(i * batch, batch)], sem.at[i]
            )
        )
        copies[-1].start()
    for copy in copies:
        copy.wait()


def correlate(parts, flips, left, scale, cw):
    quarter, columns = scale.shape
    steps = 4
    return pl.pallas_call(
        functools.partial(correlate_kernel, flips, cw),
        out_shape=jax.ShapeDtypeStruct((quarter, LAGS, columns), jnp.float32),
        in_specs=[VMEM] * (len(parts) + 2),
        out_specs=HBM,
        scratch_shapes=[
            pltpu.VMEM((columns, left.shape[1]), jnp.bfloat16),
            pltpu.VMEM((steps, quarter // steps, LAGS, columns), jnp.float32),
            pltpu.SemaphoreType.DMA((steps,)),
        ],
        compiler_params=pltpu.CompilerParams(vmem_limit_bytes=LIMIT),
        name="correlate",
    )(*parts, left, scale)


def stage_kernel(table_hbm, after_hbm, out_ref, sem):
    copy = pltpu.make_async_copy(table_hbm, out_ref, sem)
    copy.start()
    copy.wait()


def stage(table, after):
    return pl.pallas_call(
        stage_kernel,
        out_shape=jax.ShapeDtypeStruct(table.shape, table.dtype),
        in_specs=[HBM, pl.BlockSpec(memory_space=pl.ANY)],
        out_specs=VMEM,
        scratch_shapes=[pltpu.SemaphoreType.DMA(())],
        compiler_params=pltpu.CompilerParams(vmem_limit_bytes=LIMIT),
        cost_estimate=pl.CostEstimate(flops=1, bytes_accessed=4 << 20, transcendentals=0),
        name="stage",
    )(table, after)


def swap(x, axis, flip):
    size = lax.axis_size(axis)
    return lax.ppermute(x, axis, [(i, i ^ flip) for i in range(size)])


def regroup(x):
    shards_in, rows, span = x.shape
    if span == CHUNK:
        return x
    joined = jnp.transpose(x, (1, 0, 2)).reshape(rows, -1, CHUNK)
    return jnp.transpose(joined, (1, 0, 2))


def gather_sources(given, table):
    chans, chan = lax.axis_size("chan"), lax.axis_index("chan")
    windows, quarter, span = given[0].shape
    mine = given[0]
    for other in [swap(part, "rep", flip) for flip, part in enumerate(given) if flip]:
        mine = mine + other
    table = stage(table, mine)
    held = mine.reshape(1, windows * quarter, span)
    near = min(4, chans // 2)
    keys = list(range(near))
    held = jnp.concatenate([held] + [swap(held, "chan", key) for key in keys[1:]], axis=0)
    flip = near
    while flip < chans // 2:
        held = jnp.concatenate([held, swap(held, "chan", flip)], axis=0)
        keys = keys + [key ^ flip for key in keys]
        flip *= 2
    held, table = lax.optimization_barrier((held, table))
    other = swap(held, "chan", flip)
    if span == CHUNK:
        return table, (held, other), (tuple(keys), tuple(key ^ flip for key in keys))
    every = jnp.concatenate([held, other], axis=0)
    keys = jnp.asarray(keys + [key ^ flip for key in keys], jnp.int32)
    every = jnp.zeros_like(every).at[chan ^ keys].set(every)
    every = regroup(every)
    return table, (every,), ((None,) * every.shape[0],)


def shards(records, sources, dead_list):
    windows, groups, width, span = records.shape
    reps, chans = lax.axis_size("rep"), lax.axis_size("chan")
    cw = width * reps
    per = groups // chans
    blocks, *given, live, source_live, scale = pack(records, sources, dead_list, chans, reps)
    blocks = blocks.reshape(chans, windows * per * width, span)
    arrived = regroup(lax.all_to_all(blocks, "chan", 0, 0, tiled=True))
    table, parts, keys = gather_sources(given, jnp.asarray(dft_table(chans * span)))
    tables = [table, jnp.asarray(sample_band()), jnp.asarray(bin_band())]
    spectra = channel_spectra(arrived, live, tables, windows)
    left = source_kernels(parts, keys, source_live, tables, windows)
    pieces, flips = [spectra], [0]
    flip = reps // 2
    while flip:
        others = [swap(piece, "rep", flip) for piece in pieces]
        if flip > 1:
            others, left = lax.optimization_barrier((others, left))
        pieces = pieces + others
        flips = flips + [f ^ flip for f in flips]
        flip //= 2
    return correlate(pieces, flips, left, scale, cw)


def solution(mesh):
    placed = (P(None, None, "rep", "chan"), P(), P())
    return jax.shard_map(
        shards, mesh=mesh, in_specs=placed, out_specs=P("rep", None, "chan"), check_vma=False
    )
```

```python
import functools
import math

import jax
import jax.numpy as jnp
import numpy as np
from jax import lax
from jax.experimental import pallas as pl
from jax.experimental.pallas import tpu as pltpu
from jax.sharding import PartitionSpec as P

WINDOW_SAMPLES = 2048
K = 256
K0 = 16
HALF = 32
WH = 32
LAGS = 64
EPS = 1e-06

CHUNK = 256
EDGE = 128
VMEM = pl.BlockSpec(memory_space=pltpu.VMEM)
LIMIT = 16 * 1024 * 1024
WHOLE = 60 * 1024 * 1024
HBM = pl.BlockSpec(memory_space=pltpu.HBM)


def dft_table(length):
    sample = np.arange(length, dtype=np.int64)[:, None]
    bin_index = K0 + np.arange(K, dtype=np.int64)[None, :]
    angle = (sample * bin_index % length) * (2.0 * math.pi / length)
    table = np.concatenate([np.cos(angle), -np.sin(angle)], axis=1)
    return table.astype(np.float32).astype(jnp.bfloat16)


def lag_tables():
    bin_index = K0 + np.arange(K, dtype=np.int64)[None, :]
    lag = np.arange(LAGS, dtype=np.int64)[:, None] - LAGS // 2
    angle = np.mod(lag * bin_index, WINDOW_SAMPLES) * (2.0 * math.pi / WINDOW_SAMPLES)
    return np.cos(angle).astype(np.float32), np.sin(angle).astype(np.float32)


def sample_band():
    source = np.arange(CHUNK + 2 * EDGE)[:, None] - EDGE
    target = np.arange(CHUNK)[None, :]
    return (np.abs(source - target) <= HALF).astype(np.float32).astype(jnp.bfloat16)


def bin_band():
    row = np.arange(K)[:, None]
    column = np.arange(K)[None, :]
    return (np.abs(row - column) <= WH).astype(np.float32).astype(jnp.bfloat16)


def iota(shape, dim):
    return lax.broadcasted_iota(jnp.int32, shape, dim)


def columns_of(row):
    return jnp.concatenate(
        [
            jnp.broadcast_to(row[:, i : i + 128], (128, 128)).T
            for i in range(0, row.shape[1], 128)
        ],
        axis=0,
    )


def listed(ids, dead):
    hit = jnp.zeros((ids.shape[0], 128), jnp.float32)
    for i in range(0, dead.shape[1], 128):
        hit = jnp.maximum(hit, jnp.where(ids == dead[:, i : i + 128], 1.0, 0.0))
    return jnp.max(hit, axis=1, keepdims=True)


def pack_kernel(
    cw, rec_hbm, src_hbm, dead_hbm,
    out_ref, *refs,
):
    part_refs = refs[:-8]
    live_ref, source_live_ref, scale_ref, rec_ref, src_ref, dead_ref, pick_ref, sem = refs[-8:]
    copies = [
        pltpu.make_async_copy(src_hbm, src_ref, sem.at[0]),
        pltpu.make_async_copy(dead_hbm, dead_ref, sem.at[1]),
    ]
    windows, groups, width, span = rec_ref.shape
    per = groups // out_ref.shape[0]
    brought = [
        pltpu.make_async_copy(rec_hbm.at[w], rec_ref.at[w], sem.at[2 + w]) for w in range(windows)
    ]
    for copy in copies + brought:
        copy.start()
    reps = cw // width
    rep, chan = lax.axis_index("rep"), lax.axis_index("chan")
    count = src_ref.shape[1]
    quarter = count // reps
    here = pl.ds(pl.multiple_of(rep * quarter, quarter), quarter)
    copies[0].wait()
    column = columns_of(src_ref[...])
    local = groups * width
    place = iota((count, local), 1)
    ids = (place // width) * cw + rep * width + place % width
    wide = jnp.concatenate([column] * (local // 128), axis=1)
    onehot = jnp.where(wide == ids, 1.0, 0.0).astype(jnp.bfloat16)
    copies[1].wait()
    row = iota((per * width, 1), 0)
    row_ids = (chan * per + row // width) * cw + rep * width + row % width
    block_ids = chan * per * cw + iota((1, per * cw), 1)
    pairs = jnp.zeros((count, per * cw), jnp.float32)
    for w in range(windows):
        dead = dead_ref[w : w + 1, :]
        live_ref[w * per * width : (w + 1) * per * width, :] = 1.0 - listed(row_ids, dead)
        source_live = 1.0 - listed(column, dead)
        pick_ref[:, :1] = source_live
        source_live_ref[w * quarter : (w + 1) * quarter, :] = pick_ref[here, :1]
        dead_column = columns_of(dead)
        hits = [
            jnp.max(
                jnp.where(dead_column == block_ids[:, i : i + 128], 1.0, 0.0), axis=0, keepdims=True
            )
            for i in range(0, per * cw, 128)
        ]
        pairs += source_live * (1.0 - jnp.concatenate(hits, axis=1))
    for i in range(0, per * cw, span):
        pick_ref[:, : min(span, per * cw)] = pairs[:, i : i + span]
        scale_ref[:, i : i + span] = 1.0 / (
            math.sqrt(K) * jnp.maximum(pick_ref[here, : min(span, per * cw)], 1.0)
        )
    for w in range(windows):
        brought[w].wait()
        for g in range(groups):
            out_ref[g // per, w, g % per] = rec_ref[w, g]
    for w in range(windows):
        rows = rec_ref[w].reshape(local, span)
        pick_ref[...] = jnp.dot(onehot, rows, preferred_element_type=jnp.float32)
        for flip, ref in enumerate(part_refs):
            first = pl.multiple_of((rep ^ flip) * quarter, quarter)
            ref[w] = pick_ref[pl.ds(first, quarter), :].astype(jnp.bfloat16)


def pack(records, sources, dead_list, chans, reps):
    records, sources, dead_list = [pltpu.with_memory_space_constraint(a, pltpu.HBM) for a in (records, sources.reshape(1, -1), dead_list)]
    windows, groups, width, span = records.shape
    count = sources.shape[1]
    per = groups // chans
    part = jax.ShapeDtypeStruct((windows, count // reps, span), jnp.bfloat16)
    return pl.pallas_call(
        functools.partial(pack_kernel, width * reps),
        out_shape=(
            jax.ShapeDtypeStruct((chans, windows, per, width, span), jnp.bfloat16),
            *[part] * reps,
            jax.ShapeDtypeStruct((windows * per * width, 1), jnp.float32),
            jax.ShapeDtypeStruct((windows * count // reps, 1), jnp.float32),
            jax.ShapeDtypeStruct((count // reps, per * width * reps), jnp.float32),
        ),
        in_specs=[HBM] * 3,
        out_specs=(VMEM,) * (reps + 4),
        scratch_shapes=[
            pltpu.VMEM(records.shape, jnp.bfloat16),
            pltpu.VMEM((1, count), jnp.int32),
            pltpu.VMEM(dead_list.shape, jnp.int32),
            pltpu.VMEM((count, span), jnp.float32),
            pltpu.SemaphoreType.DMA((2 + windows,)),
        ],
        compiler_params=pltpu.CompilerParams(vmem_limit_bytes=LIMIT),
        name="pack",
    )(records, sources, dead_list)


def whiten_rows(x_ref, ext_ref, table_ref, band_ref, bins_ref):
    pieces, rows, _ = x_ref.shape
    length = pieces * CHUNK
    for i in range(pieces):
        here = pl.ds(i * rows, rows)
        ext_ref[here, EDGE : EDGE + CHUNK] = jnp.abs(x_ref[i])
        blank = jnp.zeros((rows, EDGE), jnp.bfloat16)
        ext_ref[here, :EDGE] = jnp.abs(x_ref[i - 1, :, CHUNK - EDGE :]) if i else blank
        ext_ref[here, EDGE + CHUNK :] = (
            jnp.abs(x_ref[i + 1, :, :EDGE]) if i < pieces - 1 else blank
        )
    totals = jnp.dot(ext_ref[...], band_ref[...], preferred_element_type=jnp.float32)
    spectrum = jnp.zeros((rows, 2 * K), jnp.float32)
    for i in range(pieces):
        sample = iota((1, CHUNK), 1) + i * CHUNK
        counts = jnp.minimum(sample, HALF) + jnp.minimum(length - 1 - sample, HALF) + 1
        mean = totals[i * rows : (i + 1) * rows] * (1.0 / counts.astype(jnp.float32))
        normed = (x_ref[i].astype(jnp.float32) / (mean + EPS)).astype(jnp.bfloat16)
        spectrum += jnp.dot(
            normed, table_ref[i * CHUNK : (i + 1) * CHUNK, :], preferred_element_type=jnp.float32
        )
    real_part, imag_part = spectrum[:, :K], spectrum[:, K:]
    amplitude = jnp.sqrt(real_part * real_part + imag_part * imag_part)
    high = amplitude.astype(jnp.bfloat16)
    rest = amplitude - high.astype(jnp.float32)
    middle = rest.astype(jnp.bfloat16)
    low = (rest - middle.astype(jnp.float32)).astype(jnp.bfloat16)
    stacked = jnp.concatenate([high, middle, low], axis=0)
    sums = jnp.dot(stacked, bins_ref[...], preferred_element_type=jnp.float32)
    place = iota((1, K), 1)
    width = jnp.minimum(place, WH) + jnp.minimum(K - 1 - place, WH) + 1
    smooth = (sums[:rows] + sums[rows : 2 * rows] + sums[2 * rows :]) * (
        1.0 / width.astype(jnp.float32)
    )
    scale = 1.0 / (smooth + EPS)
    return real_part * scale, imag_part * scale


def channel_kernel(x_ref, live_ref, table_ref, band_ref, bins_ref, out_ref, ext_ref):
    windows, count, _ = out_ref.shape
    real_part, imag_part = whiten_rows(x_ref, ext_ref, table_ref, band_ref, bins_ref)
    for w in range(windows):
        here = slice(w * count, (w + 1) * count)
        out_ref[w, :, :K] = (real_part[here] * live_ref[here, :]).astype(jnp.bfloat16)
        out_ref[w, :, K:] = (imag_part[here] * live_ref[here, :]).astype(jnp.bfloat16)


def channel_spectra(x, live, tables, windows):
    pieces, rows, _ = x.shape
    return pl.pallas_call(
        channel_kernel,
        out_shape=jax.ShapeDtypeStruct((windows, rows // windows, 2 * K), jnp.bfloat16),
        in_specs=[VMEM] * 5,
        out_specs=VMEM,
        scratch_shapes=[pltpu.VMEM((pieces * rows, CHUNK + 2 * EDGE), jnp.bfloat16)],
        compiler_params=pltpu.CompilerParams(vmem_limit_bytes=LIMIT),
        cost_estimate=pl.CostEstimate(
            flops=1, bytes_accessed=1, transcendentals=0
        ),
        name="channel_spectra",
    )(x, live, *tables)


def source_kernel(keys, *refs):
    parts = refs[: len(keys)]
    live_ref, table_ref, band_ref, bins_ref = refs[len(keys) : -3]
    out_ref, x_ref, ext_ref = refs[-3:]
    chan = lax.axis_index("chan")
    for part, slots in zip(parts, keys):
        for n, key in enumerate(slots):
            x_ref[chan ^ key if key is not None else n] = part[n]
    real_part, imag_part = whiten_rows(x_ref, ext_ref, table_ref, band_ref, bins_ref)
    out_ref[:, :K] = (real_part * live_ref[...]).astype(jnp.bfloat16)
    out_ref[:, K:] = (imag_part * live_ref[...]).astype(jnp.bfloat16)


def source_spectra(parts, keys, live, tables):
    rows = parts[0].shape[1]
    pieces = sum(len(slots) for slots in keys)
    return pl.pallas_call(
        functools.partial(source_kernel, keys),
        out_shape=jax.ShapeDtypeStruct((rows, 2 * K), jnp.bfloat16),
        in_specs=[VMEM] * (len(parts) + 4),
        out_specs=VMEM,
        scratch_shapes=[
            pltpu.VMEM((pieces, rows, CHUNK), jnp.bfloat16),
            pltpu.VMEM((pieces * rows, CHUNK + 2 * EDGE), jnp.bfloat16),
        ],
        compiler_params=pltpu.CompilerParams(vmem_limit_bytes=LIMIT),
        cost_estimate=pl.CostEstimate(flops=1 << 34, bytes_accessed=8 << 20, transcendentals=0),
        name="source_spectra",
    )(*parts, live, *tables)


def lag_kernel(windows, spec_ref, cos_ref, sin_ref, out_ref):
    spec = spec_ref[...].astype(jnp.float32)
    quarter = spec.shape[0] // windows
    lags = cos_ref.shape[0]
    for s in range(quarter):
        for w in range(windows):
            u = spec[w * quarter + s : w * quarter + s + 1, :K]
            v = spec[w * quarter + s : w * quarter + s + 1, K:]
            rows = slice(s * lags, (s + 1) * lags)
            first = w * 2 * K
            out_ref[rows, first : first + K] = (
                u * cos_ref[...] + v * sin_ref[...]
            ).astype(jnp.bfloat16)
            out_ref[rows, first + K : first + 2 * K] = (
                v * cos_ref[...] - u * sin_ref[...]
            ).astype(jnp.bfloat16)


def lag_kernels(spec, windows):
    rows = spec.shape[0]
    cosine, sine = lag_tables()
    return pl.pallas_call(
        functools.partial(lag_kernel, windows),
        out_shape=jax.ShapeDtypeStruct((rows // windows * LAGS, windows * 2 * K), jnp.bfloat16),
        in_specs=[VMEM] * 3,
        out_specs=VMEM,
        compiler_params=pltpu.CompilerParams(vmem_limit_bytes=LIMIT),
        cost_estimate=pl.CostEstimate(flops=1 << 34, bytes_accessed=8 << 20, transcendentals=0),
        name="lag_kernels",
    )(spec, jnp.asarray(cosine), jnp.asarray(sine))


def merge_kernel(*refs):
    total = refs[0][...]
    for ref in refs[1:-1]:
        total = total + ref[...]
    refs[-1][...] = total


def merge(parts):
    return pl.pallas_call(
        merge_kernel,
        out_shape=jax.ShapeDtypeStruct(parts[0].shape, parts[0].dtype),
        in_specs=[VMEM] * len(parts),
        out_specs=VMEM,
        compiler_params=pltpu.CompilerParams(vmem_limit_bytes=LIMIT),
        cost_estimate=pl.CostEstimate(flops=1, bytes_accessed=1, transcendentals=0),
        name="merge",
    )(*parts)


def correlate_kernel(flips, cw, *refs):
    parts = refs[: len(flips)]
    left_ref, scale_ref, out_hbm, right_ref, out_ref, sem = refs[len(flips) :]
    windows, count, features = parts[0].shape
    steps, batch, lags, columns = out_ref.shape
    per = columns // cw
    width = count // per
    rep = lax.axis_index("rep")
    for part, flip in zip(parts, flips):
        for w in range(windows):
            for g in range(per):
                first = pl.multiple_of(g * cw + (rep ^ flip) * width, width)
                right_ref[pl.ds(first, width), pl.ds(w * features, features)] = part[
                    w, pl.ds(g * width, width), :
                ]
    copies = []
    for i in range(steps):
        summed = lax.dot_general(
            left_ref[i * batch * lags : (i + 1) * batch * lags, :],
            right_ref[...],
            (((1,), (1,)), ((), ())),
            preferred_element_type=jnp.float32,
        )
        for n in range(batch):
            s = i * batch + n
            out_ref[i, n] = summed[n * lags : (n + 1) * lags] * scale_ref[s : s + 1, :]
        copies.append(
            pltpu.make_async_copy(
                out_ref.at[i], out_hbm.at[pl.ds(i * batch, batch)], sem.at[i]
            )
        )
        copies[-1].start()
    for copy in copies:
        copy.wait()


def correlate(parts, flips, left, scale, cw):
    quarter, columns = scale.shape
    steps = 8
    return pl.pallas_call(
        functools.partial(correlate_kernel, flips, cw),
        out_shape=jax.ShapeDtypeStruct((quarter, LAGS, columns), jnp.float32),
        in_specs=[VMEM] * (len(parts) + 2),
        out_specs=HBM,
        scratch_shapes=[
            pltpu.VMEM((columns, left.shape[1]), jnp.bfloat16),
            pltpu.VMEM((steps, quarter // steps, LAGS, columns), jnp.float32),
            pltpu.SemaphoreType.DMA((steps,)),
        ],
        compiler_params=pltpu.CompilerParams(vmem_limit_bytes=LIMIT),
        name="correlate",
    )(*parts, left, scale)


def stage_kernel(table_hbm, after_hbm, out_ref, sem):
    copy = pltpu.make_async_copy(table_hbm, out_ref, sem)
    copy.start()
    copy.wait()


def stage(table, after):
    return pl.pallas_call(
        stage_kernel,
        out_shape=jax.ShapeDtypeStruct(table.shape, table.dtype),
        in_specs=[HBM, pl.BlockSpec(memory_space=pl.ANY)],
        out_specs=VMEM,
        scratch_shapes=[pltpu.SemaphoreType.DMA(())],
        compiler_params=pltpu.CompilerParams(vmem_limit_bytes=LIMIT),
        cost_estimate=pl.CostEstimate(flops=1, bytes_accessed=4 << 20, transcendentals=0),
        name="stage",
    )(table, after)


def swap(x, axis, flip):
    size = lax.axis_size(axis)
    return lax.ppermute(x, axis, [(i, i ^ flip) for i in range(size)])


def regroup(x):
    shards_in, rows, span = x.shape
    if span == CHUNK:
        return x
    joined = jnp.transpose(x, (1, 0, 2)).reshape(rows, -1, CHUNK)
    return jnp.transpose(joined, (1, 0, 2))


def gather_sources(given, table):
    chans, chan = lax.axis_size("chan"), lax.axis_index("chan")
    windows, quarter, span = given[0].shape
    mine = merge([swap(part, "rep", flip) if flip else part for flip, part in enumerate(given)])
    table = stage(table, mine)
    held = mine.reshape(1, windows * quarter, span)
    near = min(4, chans // 2)
    keys = list(range(near))
    held = jnp.concatenate([held] + [swap(held, "chan", key) for key in keys[1:]], axis=0)
    flip = near
    while flip < chans // 2:
        held = jnp.concatenate([held, swap(held, "chan", flip)], axis=0)
        keys = keys + [key ^ flip for key in keys]
        flip *= 2
    held, table = lax.optimization_barrier((held, table))
    other = swap(held, "chan", flip)
    if span == CHUNK:
        return table, (held, other), (tuple(keys), tuple(key ^ flip for key in keys))
    every = jnp.concatenate([held, other], axis=0)
    keys = jnp.asarray(keys + [key ^ flip for key in keys], jnp.int32)
    every = jnp.zeros_like(every).at[chan ^ keys].set(every)
    every = regroup(every)
    return table, (every,), ((None,) * every.shape[0],)


def shards(records, sources, dead_list):
    windows, groups, width, span = records.shape
    reps, chans = lax.axis_size("rep"), lax.axis_size("chan")
    cw = width * reps
    per = groups // chans
    blocks, *given, live, source_live, scale = pack(records, sources, dead_list, chans, reps)
    blocks = blocks.reshape(chans, windows * per * width, span)
    arrived = regroup(lax.all_to_all(blocks, "chan", 0, 0, tiled=True))
    table, parts, keys = gather_sources(given, jnp.asarray(dft_table(chans * span)))
    tables = [table, jnp.asarray(sample_band()), jnp.asarray(bin_band())]
    spectra = channel_spectra(arrived, live, tables, windows)
    source_spec = source_spectra(parts, keys, source_live, tables)
    pieces, flips = [spectra], [0]
    flip = reps // 2
    while flip:
        others = [swap(piece, "rep", flip) for piece in pieces]
        if flip > 1:
            others, source_spec = lax.optimization_barrier((others, source_spec))
        pieces = pieces + others
        flips = flips + [f ^ flip for f in flips]
        flip //= 2
    left = lag_kernels(source_spec, windows)
    return correlate(pieces, flips, left, scale, cw)


def solution(mesh):
    placed = (P(None, None, "rep", "chan"), P(), P())
    return jax.shard_map(
        shards, mesh=mesh, in_specs=placed, out_specs=P("rep", None, "chan"), check_vma=False
    )
```

```python
import functools
import math

import jax
import jax.numpy as jnp
import numpy as np
from jax import lax
from jax.experimental import pallas as pl
from jax.experimental.pallas import tpu as pltpu
from jax.sharding import PartitionSpec as P

WINDOW_SAMPLES = 2048
K = 256
K0 = 16
HALF = 32
WH = 32
LAGS = 64
EPS = 1e-06

CHUNK = 256
EDGE = 128
ORDER = (3, 7, 6, 5, 1, 0, 4, 2)
VMEM = pl.BlockSpec(memory_space=pltpu.VMEM)
LIMIT = 16 * 1024 * 1024
STAGE_FLOPS = 1
HBM = pl.BlockSpec(memory_space=pltpu.HBM)


def dft_table(length):
    sample = np.arange(length, dtype=np.int64)[:, None]
    bin_index = K0 + np.arange(K, dtype=np.int64)[None, :]
    angle = (sample * bin_index % length) * (2.0 * math.pi / length)
    table = np.concatenate([np.cos(angle), -np.sin(angle)], axis=1)
    return table.astype(np.float32).astype(jnp.bfloat16)


def lag_tables():
    bin_index = K0 + np.arange(K, dtype=np.int64)[None, :]
    lag = np.arange(LAGS, dtype=np.int64)[:, None] - LAGS // 2
    angle = np.mod(lag * bin_index, WINDOW_SAMPLES) * (2.0 * math.pi / WINDOW_SAMPLES)
    return np.cos(angle).astype(np.float32), np.sin(angle).astype(np.float32)


def sample_band():
    source = np.arange(CHUNK + 2 * EDGE)[:, None] - EDGE
    target = np.arange(CHUNK)[None, :]
    return (np.abs(source - target) <= HALF).astype(np.float32).astype(jnp.bfloat16)


def bin_band():
    row = np.arange(K)[:, None]
    column = np.arange(K)[None, :]
    return (np.abs(row - column) <= WH).astype(np.float32).astype(jnp.bfloat16)


def order_of(chans):
    return ORDER if chans == len(ORDER) else tuple(range(chans))


def iota(shape, dim):
    return lax.broadcasted_iota(jnp.int32, shape, dim)


def columns_of(row):
    return jnp.concatenate(
        [
            jnp.broadcast_to(row[:, i : i + 128], (128, 128)).T
            for i in range(0, row.shape[1], 128)
        ],
        axis=0,
    )


def listed(ids, dead):
    hit = jnp.zeros((ids.shape[0], 128), jnp.float32)
    for i in range(0, dead.shape[1], 128):
        hit = jnp.maximum(hit, jnp.where(ids == dead[:, i : i + 128], 1.0, 0.0))
    return jnp.max(hit, axis=1, keepdims=True)


def pack_kernel(cw, rec_hbm, src_hbm, out_ref, *refs):
    *low_refs, high_ref, src_ref, pick_ref, sem = refs
    windows, groups, width, span = rec_hbm.shape
    per = groups // out_ref.shape[0]
    order = order_of(out_ref.shape[0])
    brought = pltpu.make_async_copy(src_hbm, src_ref, sem.at[windows, 0])
    brought.start()
    copies = []
    for w in range(windows):
        copies.append(
            [
                pltpu.make_async_copy(
                    rec_hbm.at[w, pl.ds(member * per, per)], out_ref.at[n, w], sem.at[w, n]
                )
                for n, member in enumerate(order)
            ]
        )
        for copy in copies[-1]:
            copy.start()
    reps = cw // width
    rep = lax.axis_index("rep")
    count = src_ref.shape[1]
    quarter = count // reps
    local = groups * width
    place = iota((count, local), 1)
    ids = (place // width) * cw + rep * width + place % width
    brought.wait()
    wide = jnp.concatenate([columns_of(src_ref[...])] * (local // 128), axis=1)
    onehot = jnp.where(wide == ids, 1.0, 0.0).astype(jnp.bfloat16)
    for w in range(windows):
        for copy in copies[w]:
            copy.wait()
        rows = jnp.concatenate(
            [out_ref[order.index(g // per), w, g % per] for g in range(groups)], axis=0
        )
        pick_ref[...] = jnp.dot(onehot, rows, preferred_element_type=jnp.float32)
        for flip in range(reps):
            first = pl.multiple_of((rep ^ flip) * quarter, quarter)
            picked = pick_ref[pl.ds(first, quarter), :].astype(jnp.bfloat16)
            if flip < reps // 2:
                low_refs[flip][w] = picked
            else:
                high_ref[flip - reps // 2, w] = picked


def in_hbm(*arrays):
    return [pltpu.with_memory_space_constraint(array, pltpu.HBM) for array in arrays]


def pack(records, sources, chans, reps):
    windows, groups, width, span = records.shape
    count = sources.shape[0]
    per = groups // chans
    part = (windows, count // reps, span)
    return pl.pallas_call(
        functools.partial(pack_kernel, width * reps),
        out_shape=(
            jax.ShapeDtypeStruct((chans, windows, per, width, span), jnp.bfloat16),
            *[jax.ShapeDtypeStruct(part, jnp.bfloat16)] * (reps // 2),
            jax.ShapeDtypeStruct((reps // 2,) + part, jnp.bfloat16),
        ),
        in_specs=[HBM] * 2,
        out_specs=(VMEM,) * (reps // 2 + 2),
        scratch_shapes=[
            pltpu.VMEM((1, count), jnp.int32),
            pltpu.VMEM((count, span), jnp.float32),
            pltpu.SemaphoreType.DMA((1 + windows, chans)),
        ],
        compiler_params=pltpu.CompilerParams(vmem_limit_bytes=LIMIT),
        name="pack",
    )(*in_hbm(records, sources.reshape(1, count)))


def stage_kernel(
    cw, width, table_hbm, src_hbm, dead_hbm, after_hbm,
    table_ref, live_ref, source_live_ref, scale_ref,
    src_ref, dead_ref, pick_ref, sem,
):
    copies = [
        pltpu.make_async_copy(src_hbm, src_ref, sem.at[0]),
        pltpu.make_async_copy(dead_hbm, dead_ref, sem.at[1]),
        pltpu.make_async_copy(table_hbm, table_ref, sem.at[2]),
    ]
    for copy in copies:
        copy.start()
    windows = dead_ref.shape[0]
    rep, chan = lax.axis_index("rep"), lax.axis_index("chan")
    count = src_ref.shape[1]
    quarter, columns = scale_ref.shape
    per = columns // cw
    here = pl.ds(pl.multiple_of(rep * quarter, quarter), quarter)
    row = iota((per * width, 1), 0)
    row_ids = (chan * per + row // width) * cw + rep * width + row % width
    block_ids = chan * columns + iota((1, columns), 1)
    copies[0].wait()
    copies[1].wait()
    column = columns_of(src_ref[...])
    pick_ref[...] = column
    mine = pick_ref[here, :]
    pairs = jnp.zeros((quarter, columns), jnp.float32)
    for w in range(windows):
        dead = dead_ref[w : w + 1, :]
        live_ref[w * per * width : (w + 1) * per * width, :] = 1.0 - listed(row_ids, dead)
        source_live = 1.0 - listed(mine, dead)
        source_live_ref[w * quarter : (w + 1) * quarter, :] = source_live
        dead_column = columns_of(dead)
        hits = [
            jnp.max(
                jnp.where(dead_column == block_ids[:, i : i + 128], 1.0, 0.0), axis=0, keepdims=True
            )
            for i in range(0, columns, 128)
        ]
        pairs += source_live * (1.0 - jnp.concatenate(hits, axis=1))
    scale_ref[...] = 1.0 / (math.sqrt(K) * jnp.maximum(pairs, 1.0))
    copies[2].wait()


def stage(table, sources, dead_list, after, per, cw, width):
    windows = dead_list.shape[0]
    count = sources.shape[0]
    quarter = count // (cw // width)
    return pl.pallas_call(
        functools.partial(stage_kernel, cw, width),
        out_shape=(
            jax.ShapeDtypeStruct(table.shape, table.dtype),
            jax.ShapeDtypeStruct((windows * per * width, 1), jnp.float32),
            jax.ShapeDtypeStruct((windows * quarter, 1), jnp.float32),
            jax.ShapeDtypeStruct((quarter, per * cw), jnp.float32),
        ),
        in_specs=[HBM] * 3 + [pl.BlockSpec(memory_space=pl.ANY)],
        out_specs=(VMEM,) * 4,
        scratch_shapes=[
            pltpu.VMEM((1, count), jnp.int32),
            pltpu.VMEM(dead_list.shape, jnp.int32),
            pltpu.VMEM((count, 128), jnp.int32),
            pltpu.SemaphoreType.DMA((3,)),
        ],
        compiler_params=pltpu.CompilerParams(vmem_limit_bytes=LIMIT),
        cost_estimate=pl.CostEstimate(
            flops=STAGE_FLOPS, bytes_accessed=4 << 20, transcendentals=0
        ),
        name="stage",
    )(*in_hbm(table, sources.reshape(1, count), dead_list), after)


def whiten_rows(x_ref, order, ext_ref, table_ref, band_ref, bins_ref):
    pieces, rows, _ = x_ref.shape
    x = [x_ref.at[order.index(i)] for i in range(pieces)]
    length = pieces * CHUNK
    for i in range(pieces):
        here = pl.ds(i * rows, rows)
        ext_ref[here, EDGE : EDGE + CHUNK] = jnp.abs(x[i][...])
        blank = jnp.zeros((rows, EDGE), jnp.bfloat16)
        ext_ref[here, :EDGE] = jnp.abs(x[i - 1][:, CHUNK - EDGE :]) if i else blank
        ext_ref[here, EDGE + CHUNK :] = (
            jnp.abs(x[i + 1][:, :EDGE]) if i < pieces - 1 else blank
        )
    totals = jnp.dot(ext_ref[...], band_ref[...], preferred_element_type=jnp.float32)
    spectrum = jnp.zeros((rows, 2 * K), jnp.float32)
    for i in range(pieces):
        sample = iota((1, CHUNK), 1) + i * CHUNK
        counts = jnp.minimum(sample, HALF) + jnp.minimum(length - 1 - sample, HALF) + 1
        mean = totals[i * rows : (i + 1) * rows] * (1.0 / counts.astype(jnp.float32))
        normed = (x[i][...].astype(jnp.float32) / (mean + EPS)).astype(jnp.bfloat16)
        spectrum += jnp.dot(
            normed, table_ref[i * CHUNK : (i + 1) * CHUNK, :], preferred_element_type=jnp.float32
        )
    real_part, imag_part = spectrum[:, :K], spectrum[:, K:]
    amplitude = jnp.sqrt(real_part * real_part + imag_part * imag_part)
    high = amplitude.astype(jnp.bfloat16)
    rest = amplitude - high.astype(jnp.float32)
    middle = rest.astype(jnp.bfloat16)
    low = (rest - middle.astype(jnp.float32)).astype(jnp.bfloat16)
    stacked = jnp.concatenate([high, middle, low], axis=0)
    sums = jnp.dot(stacked, bins_ref[...], preferred_element_type=jnp.float32)
    place = iota((1, K), 1)
    width = jnp.minimum(place, WH) + jnp.minimum(K - 1 - place, WH) + 1
    smooth = (sums[:rows] + sums[rows : 2 * rows] + sums[2 * rows :]) * (
        1.0 / width.astype(jnp.float32)
    )
    scale = 1.0 / (smooth + EPS)
    return real_part * scale, imag_part * scale


def channel_kernel(order, x_ref, live_ref, table_ref, band_ref, bins_ref, out_ref, ext_ref):
    windows, count, _ = out_ref.shape
    real_part, imag_part = whiten_rows(x_ref, order, ext_ref, table_ref, band_ref, bins_ref)
    for w in range(windows):
        here = slice(w * count, (w + 1) * count)
        out_ref[w, :, :K] = (real_part[here] * live_ref[here, :]).astype(jnp.bfloat16)
        out_ref[w, :, K:] = (imag_part[here] * live_ref[here, :]).astype(jnp.bfloat16)


def channel_spectra(x, order, live, tables, windows):
    pieces, rows, _ = x.shape
    return pl.pallas_call(
        functools.partial(channel_kernel, order),
        out_shape=jax.ShapeDtypeStruct((windows, rows // windows, 2 * K), jnp.bfloat16),
        in_specs=[VMEM] * 5,
        out_specs=VMEM,
        scratch_shapes=[pltpu.VMEM((pieces * rows, CHUNK + 2 * EDGE), jnp.bfloat16)],
        compiler_params=pltpu.CompilerParams(vmem_limit_bytes=LIMIT),
        cost_estimate=pl.CostEstimate(
            flops=1, bytes_accessed=1, transcendentals=0
        ),
        name="channel_spectra",
    )(x, live, *tables)


def source_kernel(keys, *refs):
    parts = refs[: len(keys)]
    live_ref, table_ref, band_ref, bins_ref = refs[len(keys) : -3]
    out_ref, x_ref, ext_ref = refs[-3:]
    chan = lax.axis_index("chan")
    for part, slots in zip(parts, keys):
        for n, key in enumerate(slots):
            x_ref[chan ^ key if key is not None else n] = part[n]
    order = tuple(range(x_ref.shape[0]))
    real_part, imag_part = whiten_rows(x_ref, order, ext_ref, table_ref, band_ref, bins_ref)
    out_ref[:, :K] = (real_part * live_ref[...]).astype(jnp.bfloat16)
    out_ref[:, K:] = (imag_part * live_ref[...]).astype(jnp.bfloat16)


def source_spectra(parts, keys, live, tables):
    rows = parts[0].shape[1]
    pieces = sum(len(slots) for slots in keys)
    return pl.pallas_call(
        functools.partial(source_kernel, keys),
        out_shape=jax.ShapeDtypeStruct((rows, 2 * K), jnp.bfloat16),
        in_specs=[VMEM] * (len(parts) + 4),
        out_specs=VMEM,
        scratch_shapes=[
            pltpu.VMEM((pieces, rows, CHUNK), jnp.bfloat16),
            pltpu.VMEM((pieces * rows, CHUNK + 2 * EDGE), jnp.bfloat16),
        ],
        compiler_params=pltpu.CompilerParams(vmem_limit_bytes=LIMIT),
        cost_estimate=pl.CostEstimate(flops=1 << 34, bytes_accessed=8 << 20, transcendentals=0),
        name="source_spectra",
    )(*parts, live, *tables)


def lag_kernel(windows, spec_ref, cos_ref, sin_ref, out_ref):
    spec = spec_ref[...].astype(jnp.float32)
    quarter = spec.shape[0] // windows
    lags = cos_ref.shape[0]
    for s in range(quarter):
        for w in range(windows):
            u = spec[w * quarter + s : w * quarter + s + 1, :K]
            v = spec[w * quarter + s : w * quarter + s + 1, K:]
            rows = slice(s * lags, (s + 1) * lags)
            first = w * 2 * K
            out_ref[rows, first : first + K] = (
                u * cos_ref[...] + v * sin_ref[...]
            ).astype(jnp.bfloat16)
            out_ref[rows, first + K : first + 2 * K] = (
                v * cos_ref[...] - u * sin_ref[...]
            ).astype(jnp.bfloat16)


def lag_kernels(spec, windows):
    rows = spec.shape[0]
    cosine, sine = lag_tables()
    return pl.pallas_call(
        functools.partial(lag_kernel, windows),
        out_shape=jax.ShapeDtypeStruct((rows // windows * LAGS, windows * 2 * K), jnp.bfloat16),
        in_specs=[VMEM] * 3,
        out_specs=VMEM,
        compiler_params=pltpu.CompilerParams(vmem_limit_bytes=LIMIT),
        cost_estimate=pl.CostEstimate(flops=1 << 34, bytes_accessed=8 << 20, transcendentals=0),
        name="lag_kernels",
    )(spec, jnp.asarray(cosine), jnp.asarray(sine))


def correlate_kernel(flips, cw, *refs):
    parts = refs[: len(flips)]
    left_ref, scale_ref, out_hbm, right_ref, out_ref, sem = refs[len(flips) :]
    windows, count, features = parts[0].shape
    steps, batch, lags, columns = out_ref.shape
    per = columns // cw
    width = count // per
    rep = lax.axis_index("rep")
    for part, flip in zip(parts, flips):
        for w in range(windows):
            for g in range(per):
                first = pl.multiple_of(g * cw + (rep ^ flip) * width, width)
                right_ref[pl.ds(first, width), pl.ds(w * features, features)] = part[
                    w, pl.ds(g * width, width), :
                ]
    copies = []
    for i in range(steps):
        summed = lax.dot_general(
            left_ref[i * batch * lags : (i + 1) * batch * lags, :],
            right_ref[...],
            (((1,), (1,)), ((), ())),
            preferred_element_type=jnp.float32,
        )
        for n in range(batch):
            s = i * batch + n
            out_ref[i, n] = summed[n * lags : (n + 1) * lags] * scale_ref[s : s + 1, :]
        copies.append(
            pltpu.make_async_copy(
                out_ref.at[i], out_hbm.at[pl.ds(i * batch, batch)], sem.at[i]
            )
        )
        copies[-1].start()
    for copy in copies:
        copy.wait()


def correlate(parts, flips, left, scale, cw):
    quarter, columns = scale.shape
    steps = 8
    return pl.pallas_call(
        functools.partial(correlate_kernel, flips, cw),
        out_shape=jax.ShapeDtypeStruct((quarter, LAGS, columns), jnp.float32),
        in_specs=[VMEM] * (len(parts) + 2),
        out_specs=HBM,
        scratch_shapes=[
            pltpu.VMEM((columns, left.shape[1]), jnp.bfloat16),
            pltpu.VMEM((steps, quarter // steps, LAGS, columns), jnp.float32),
            pltpu.SemaphoreType.DMA((steps,)),
        ],
        compiler_params=pltpu.CompilerParams(vmem_limit_bytes=LIMIT),
        name="correlate",
    )(*parts, left, scale)


def swap(x, axis, flip):
    size = lax.axis_size(axis)
    return lax.ppermute(x, axis, [(i, i ^ flip) for i in range(size)])


def regroup(x):
    shards_in, rows, span = x.shape
    if span == CHUNK:
        return x
    joined = jnp.transpose(x, (1, 0, 2)).reshape(rows, -1, CHUNK)
    return jnp.transpose(joined, (1, 0, 2))


def gather_sources(low, high, prepare):
    chans, chan = lax.axis_size("chan"), lax.axis_index("chan")
    windows, quarter, span = low[0].shape
    flip = len(low)
    while flip:
        came = swap(high, "rep", flip)
        low = [part + came[n] for n, part in enumerate(low)]
        flip //= 2
        if flip:
            high = jnp.stack(low[flip:])
            low = low[:flip]
    mine = low[0]
    prepared = prepare(mine)
    held = mine.reshape(1, windows * quarter, span)
    near = min(4, chans // 2)
    keys = list(range(near))
    held = jnp.concatenate([held] + [swap(held, "chan", key) for key in keys[1:]], axis=0)
    flip = near
    while flip < chans // 2:
        held = jnp.concatenate([held, swap(held, "chan", flip)], axis=0)
        keys = keys + [key ^ flip for key in keys]
        flip *= 2
    held, prepared = lax.optimization_barrier((held, prepared))
    other = swap(held, "chan", flip)
    if span == CHUNK:
        return prepared, (held, other), (tuple(keys), tuple(key ^ flip for key in keys))
    every = jnp.concatenate([held, other], axis=0)
    keys = jnp.asarray(keys + [key ^ flip for key in keys], jnp.int32)
    every = jnp.zeros_like(every).at[chan ^ keys].set(every)
    every = regroup(every)
    return prepared, (every,), ((None,) * every.shape[0],)


def shards(records, sources, dead_list):
    windows, groups, width, span = records.shape
    reps, chans = lax.axis_size("rep"), lax.axis_size("chan")
    cw = width * reps
    per = groups // chans
    blocks, *low, high = pack(records, sources, chans, reps)
    blocks = blocks.reshape(chans, windows * per * width, span)
    order = order_of(chans)
    arrived = lax.all_to_all(blocks, "chan", 0, 0, axis_index_groups=[list(order)], tiled=True)
    if span != CHUNK:
        arrived = regroup(jnp.stack([arrived[order.index(i)] for i in range(chans)]))
        order = tuple(range(arrived.shape[0]))
    table = jnp.asarray(dft_table(chans * span))

    def prepare(after):
        return stage(table, sources, dead_list, after, per, cw, width)

    (table, live, source_live, scale), parts, keys = gather_sources(low, high, prepare)
    tables = [table, jnp.asarray(sample_band()), jnp.asarray(bin_band())]
    spectra = channel_spectra(arrived, order, live, tables, windows)
    source_spec = source_spectra(parts, keys, source_live, tables)
    pieces, flips = [spectra], [0]
    flip = reps // 2
    while flip:
        others = [swap(piece, "rep", flip) for piece in pieces]
        pieces = pieces + others
        flips = flips + [f ^ flip for f in flips]
        flip //= 2
    left = lag_kernels(source_spec, windows)
    return correlate(pieces, flips, left, scale, cw)


def solution(mesh):
    placed = (P(None, None, "rep", "chan"), P(), P())
    return jax.shard_map(
        shards, mesh=mesh, in_specs=placed, out_specs=P("rep", None, "chan"), check_vma=False
    )
```

```python
import functools
import math

import jax
import jax.numpy as jnp
import numpy as np
from jax import lax
from jax.experimental import pallas as pl
from jax.experimental.pallas import tpu as pltpu
from jax.sharding import PartitionSpec as P

WINDOW_SAMPLES = 2048
K = 256
K0 = 16
HALF = 32
WH = 32
LAGS = 64
EPS = 1e-06

CHUNK = 256
EDGE = 128
ORDER = (3, 6, 1, 2, 7, 0, 5, 4)
VMEM = pl.BlockSpec(memory_space=pltpu.VMEM)
LIMIT = 16 * 1024 * 1024
STAGE_FLOPS = 1
HBM = pl.BlockSpec(memory_space=pltpu.HBM)


def dft_table(length):
    sample = np.arange(length, dtype=np.int64)[:, None]
    bin_index = K0 + np.arange(K, dtype=np.int64)[None, :]
    angle = (sample * bin_index % length) * (2.0 * math.pi / length)
    table = np.concatenate([np.cos(angle), -np.sin(angle)], axis=1)
    return table.astype(np.float32).astype(jnp.bfloat16)


def lag_tables():
    bin_index = K0 + np.arange(K, dtype=np.int64)[None, :]
    lag = np.arange(LAGS, dtype=np.int64)[:, None] - LAGS // 2
    angle = np.mod(lag * bin_index, WINDOW_SAMPLES) * (2.0 * math.pi / WINDOW_SAMPLES)
    return np.cos(angle).astype(np.float32), np.sin(angle).astype(np.float32)


def sample_band():
    source = np.arange(CHUNK + 2 * EDGE)[:, None] - EDGE
    target = np.arange(CHUNK)[None, :]
    return (np.abs(source - target) <= HALF).astype(np.float32).astype(jnp.bfloat16)


def bin_band():
    row = np.arange(K)[:, None]
    column = np.arange(K)[None, :]
    return (np.abs(row - column) <= WH).astype(np.float32).astype(jnp.bfloat16)


def order_of(chans):
    return ORDER if chans == len(ORDER) else tuple(range(chans))


def iota(shape, dim):
    return lax.broadcasted_iota(jnp.int32, shape, dim)


def columns_of(row):
    return jnp.concatenate(
        [
            jnp.broadcast_to(row[:, i : i + 128], (128, 128)).T
            for i in range(0, row.shape[1], 128)
        ],
        axis=0,
    )


def listed(ids, dead):
    hit = jnp.zeros((ids.shape[0], 128), jnp.float32)
    for i in range(0, dead.shape[1], 128):
        hit = jnp.maximum(hit, jnp.where(ids == dead[:, i : i + 128], 1.0, 0.0))
    return jnp.max(hit, axis=1, keepdims=True)


def pack_kernel(cw, rec_hbm, src_hbm, out_ref, *refs):
    *low_refs, high_ref, src_ref, pick_ref, sem = refs
    windows, groups, width, span = rec_hbm.shape
    per = groups // out_ref.shape[0]
    order = order_of(out_ref.shape[0])
    brought = pltpu.make_async_copy(src_hbm, src_ref, sem.at[windows, 0])
    brought.start()
    copies = []
    for w in range(windows):
        copies.append(
            [
                pltpu.make_async_copy(
                    rec_hbm.at[w, pl.ds(member * per, per)], out_ref.at[n, w], sem.at[w, n]
                )
                for n, member in enumerate(order)
            ]
        )
        for copy in copies[-1]:
            copy.start()
    reps = cw // width
    rep = lax.axis_index("rep")
    count = src_ref.shape[1]
    quarter = count // reps
    local = groups * width
    place = iota((count, local), 1)
    ids = (place // width) * cw + rep * width + place % width
    brought.wait()
    wide = jnp.concatenate([columns_of(src_ref[...])] * (local // 128), axis=1)
    onehot = jnp.where(wide == ids, 1.0, 0.0).astype(jnp.bfloat16)
    for w in range(windows):
        for copy in copies[w]:
            copy.wait()
        rows = jnp.concatenate(
            [out_ref[order.index(g // per), w, g % per] for g in range(groups)], axis=0
        )
        pick_ref[...] = jnp.dot(onehot, rows, preferred_element_type=jnp.float32)
        for flip in range(reps):
            first = pl.multiple_of((rep ^ flip) * quarter, quarter)
            picked = pick_ref[pl.ds(first, quarter), :].astype(jnp.bfloat16)
            if flip < reps // 2:
                low_refs[flip][w] = picked
            else:
                high_ref[flip - reps // 2, w] = picked


def in_hbm(*arrays):
    return [pltpu.with_memory_space_constraint(array, pltpu.HBM) for array in arrays]


def pack(records, sources, chans, reps):
    windows, groups, width, span = records.shape
    count = sources.shape[0]
    per = groups // chans
    part = (windows, count // reps, span)
    return pl.pallas_call(
        functools.partial(pack_kernel, width * reps),
        out_shape=(
            jax.ShapeDtypeStruct((chans, windows, per, width, span), jnp.bfloat16),
            *[jax.ShapeDtypeStruct(part, jnp.bfloat16)] * (reps // 2),
            jax.ShapeDtypeStruct((reps // 2,) + part, jnp.bfloat16),
        ),
        in_specs=[HBM] * 2,
        out_specs=(VMEM,) * (reps // 2 + 2),
        scratch_shapes=[
            pltpu.VMEM((1, count), jnp.int32),
            pltpu.VMEM((count, span), jnp.float32),
            pltpu.SemaphoreType.DMA((1 + windows, chans)),
        ],
        compiler_params=pltpu.CompilerParams(vmem_limit_bytes=LIMIT),
        name="pack",
    )(*in_hbm(records, sources.reshape(1, count)))


def stage_kernel(
    cw, width, table_hbm, src_hbm, dead_hbm, after_hbm,
    table_ref, live_ref, source_live_ref, scale_ref,
    src_ref, dead_ref, pick_ref, sem,
):
    copies = [
        pltpu.make_async_copy(src_hbm, src_ref, sem.at[0]),
        pltpu.make_async_copy(dead_hbm, dead_ref, sem.at[1]),
        pltpu.make_async_copy(table_hbm, table_ref, sem.at[2]),
    ]
    for copy in copies:
        copy.start()
    windows = dead_ref.shape[0]
    rep, chan = lax.axis_index("rep"), lax.axis_index("chan")
    count = src_ref.shape[1]
    quarter, columns = scale_ref.shape
    per = columns // cw
    here = pl.ds(pl.multiple_of(rep * quarter, quarter), quarter)
    row = iota((per * width, 1), 0)
    row_ids = (chan * per + row // width) * cw + rep * width + row % width
    block_ids = chan * columns + iota((1, columns), 1)
    copies[0].wait()
    copies[1].wait()
    column = columns_of(src_ref[...])
    pick_ref[...] = column
    mine = pick_ref[here, :]
    pairs = jnp.zeros((quarter, columns), jnp.float32)
    for w in range(windows):
        dead = dead_ref[w : w + 1, :]
        live_ref[w * per * width : (w + 1) * per * width, :] = 1.0 - listed(row_ids, dead)
        source_live = 1.0 - listed(mine, dead)
        source_live_ref[w * quarter : (w + 1) * quarter, :] = source_live
        dead_column = columns_of(dead)
        hits = [
            jnp.max(
                jnp.where(dead_column == block_ids[:, i : i + 128], 1.0, 0.0), axis=0, keepdims=True
            )
            for i in range(0, columns, 128)
        ]
        pairs += source_live * (1.0 - jnp.concatenate(hits, axis=1))
    scale_ref[...] = 1.0 / (math.sqrt(K) * jnp.maximum(pairs, 1.0))
    copies[2].wait()


def stage(table, sources, dead_list, after, per, cw, width):
    windows = dead_list.shape[0]
    count = sources.shape[0]
    quarter = count // (cw // width)
    return pl.pallas_call(
        functools.partial(stage_kernel, cw, width),
        out_shape=(
            jax.ShapeDtypeStruct(table.shape, table.dtype),
            jax.ShapeDtypeStruct((windows * per * width, 1), jnp.float32),
            jax.ShapeDtypeStruct((windows * quarter, 1), jnp.float32),
            jax.ShapeDtypeStruct((quarter, per * cw), jnp.float32),
        ),
        in_specs=[HBM] * 3 + [pl.BlockSpec(memory_space=pl.ANY)],
        out_specs=(VMEM,) * 4,
        scratch_shapes=[
            pltpu.VMEM((1, count), jnp.int32),
            pltpu.VMEM(dead_list.shape, jnp.int32),
            pltpu.VMEM((count, 128), jnp.int32),
            pltpu.SemaphoreType.DMA((3,)),
        ],
        compiler_params=pltpu.CompilerParams(vmem_limit_bytes=LIMIT),
        cost_estimate=pl.CostEstimate(
            flops=STAGE_FLOPS, bytes_accessed=4 << 20, transcendentals=0
        ),
        name="stage",
    )(*in_hbm(table, sources.reshape(1, count), dead_list), after)


def whiten_rows(x_ref, order, ext_ref, table_ref, band_ref, bins_ref):
    pieces, rows, _ = x_ref.shape
    x = [x_ref.at[order.index(i)] for i in range(pieces)]
    length = pieces * CHUNK
    for i in range(pieces):
        here = pl.ds(i * rows, rows)
        ext_ref[here, EDGE : EDGE + CHUNK] = jnp.abs(x[i][...])
        blank = jnp.zeros((rows, EDGE), jnp.bfloat16)
        ext_ref[here, :EDGE] = jnp.abs(x[i - 1][:, CHUNK - EDGE :]) if i else blank
        ext_ref[here, EDGE + CHUNK :] = (
            jnp.abs(x[i + 1][:, :EDGE]) if i < pieces - 1 else blank
        )
    totals = jnp.dot(ext_ref[...], band_ref[...], preferred_element_type=jnp.float32)
    spectrum = jnp.zeros((rows, 2 * K), jnp.float32)
    for i in range(pieces):
        sample = iota((1, CHUNK), 1) + i * CHUNK
        counts = jnp.minimum(sample, HALF) + jnp.minimum(length - 1 - sample, HALF) + 1
        mean = totals[i * rows : (i + 1) * rows] * (1.0 / counts.astype(jnp.float32))
        normed = (x[i][...].astype(jnp.float32) / (mean + EPS)).astype(jnp.bfloat16)
        spectrum += jnp.dot(
            normed, table_ref[i * CHUNK : (i + 1) * CHUNK, :], preferred_element_type=jnp.float32
        )
    real_part, imag_part = spectrum[:, :K], spectrum[:, K:]
    amplitude = jnp.sqrt(real_part * real_part + imag_part * imag_part)
    high = amplitude.astype(jnp.bfloat16)
    rest = amplitude - high.astype(jnp.float32)
    middle = rest.astype(jnp.bfloat16)
    low = (rest - middle.astype(jnp.float32)).astype(jnp.bfloat16)
    stacked = jnp.concatenate([high, middle, low], axis=0)
    sums = jnp.dot(stacked, bins_ref[...], preferred_element_type=jnp.float32)
    place = iota((1, K), 1)
    width = jnp.minimum(place, WH) + jnp.minimum(K - 1 - place, WH) + 1
    smooth = (sums[:rows] + sums[rows : 2 * rows] + sums[2 * rows :]) * (
        1.0 / width.astype(jnp.float32)
    )
    scale = 1.0 / (smooth + EPS)
    return real_part * scale, imag_part * scale


def channel_kernel(order, x_ref, live_ref, table_ref, band_ref, bins_ref, out_ref, ext_ref):
    windows, count, _ = out_ref.shape
    real_part, imag_part = whiten_rows(x_ref, order, ext_ref, table_ref, band_ref, bins_ref)
    for w in range(windows):
        here = slice(w * count, (w + 1) * count)
        out_ref[w, :, :K] = (real_part[here] * live_ref[here, :]).astype(jnp.bfloat16)
        out_ref[w, :, K:] = (imag_part[here] * live_ref[here, :]).astype(jnp.bfloat16)


def channel_spectra(x, order, live, tables, windows):
    pieces, rows, _ = x.shape
    return pl.pallas_call(
        functools.partial(channel_kernel, order),
        out_shape=jax.ShapeDtypeStruct((windows, rows // windows, 2 * K), jnp.bfloat16),
        in_specs=[VMEM] * 5,
        out_specs=VMEM,
        scratch_shapes=[pltpu.VMEM((pieces * rows, CHUNK + 2 * EDGE), jnp.bfloat16)],
        compiler_params=pltpu.CompilerParams(vmem_limit_bytes=LIMIT),
        cost_estimate=pl.CostEstimate(
            flops=1, bytes_accessed=1, transcendentals=0
        ),
        name="channel_spectra",
    )(x, live, *tables)


def source_kernel(keys, *refs):
    parts = refs[: len(keys)]
    live_ref, table_ref, band_ref, bins_ref = refs[len(keys) : -3]
    out_ref, x_ref, ext_ref = refs[-3:]
    chan = lax.axis_index("chan")
    for part, slots in zip(parts, keys):
        for n, key in enumerate(slots):
            x_ref[chan ^ key if key is not None else n] = part[n]
    order = tuple(range(x_ref.shape[0]))
    real_part, imag_part = whiten_rows(x_ref, order, ext_ref, table_ref, band_ref, bins_ref)
    out_ref[:, :K] = (real_part * live_ref[...]).astype(jnp.bfloat16)
    out_ref[:, K:] = (imag_part * live_ref[...]).astype(jnp.bfloat16)


def source_spectra(parts, keys, live, tables):
    rows = parts[0].shape[1]
    pieces = sum(len(slots) for slots in keys)
    return pl.pallas_call(
        functools.partial(source_kernel, keys),
        out_shape=jax.ShapeDtypeStruct((rows, 2 * K), jnp.bfloat16),
        in_specs=[VMEM] * (len(parts) + 4),
        out_specs=VMEM,
        scratch_shapes=[
            pltpu.VMEM((pieces, rows, CHUNK), jnp.bfloat16),
            pltpu.VMEM((pieces * rows, CHUNK + 2 * EDGE), jnp.bfloat16),
        ],
        compiler_params=pltpu.CompilerParams(vmem_limit_bytes=LIMIT),
        cost_estimate=pl.CostEstimate(flops=1 << 34, bytes_accessed=8 << 20, transcendentals=0),
        name="source_spectra",
    )(*parts, live, *tables)


def lag_kernel(windows, spec_ref, cos_ref, sin_ref, out_ref):
    spec = spec_ref[...].astype(jnp.float32)
    quarter = spec.shape[0] // windows
    lags = cos_ref.shape[0]
    for s in range(quarter):
        for w in range(windows):
            u = spec[w * quarter + s : w * quarter + s + 1, :K]
            v = spec[w * quarter + s : w * quarter + s + 1, K:]
            rows = slice(s * lags, (s + 1) * lags)
            first = w * 2 * K
            out_ref[rows, first : first + K] = (
                u * cos_ref[...] + v * sin_ref[...]
            ).astype(jnp.bfloat16)
            out_ref[rows, first + K : first + 2 * K] = (
                v * cos_ref[...] - u * sin_ref[...]
            ).astype(jnp.bfloat16)


def lag_kernels(spec, windows):
    rows = spec.shape[0]
    cosine, sine = lag_tables()
    return pl.pallas_call(
        functools.partial(lag_kernel, windows),
        out_shape=jax.ShapeDtypeStruct((rows // windows * LAGS, windows * 2 * K), jnp.bfloat16),
        in_specs=[VMEM] * 3,
        out_specs=VMEM,
        compiler_params=pltpu.CompilerParams(vmem_limit_bytes=LIMIT),
        cost_estimate=pl.CostEstimate(flops=1 << 34, bytes_accessed=8 << 20, transcendentals=0),
        name="lag_kernels",
    )(spec, jnp.asarray(cosine), jnp.asarray(sine))


def correlate_kernel(flips, cw, *refs):
    parts = refs[: len(flips)]
    left_ref, scale_ref, out_hbm, right_ref, out_ref, sem = refs[len(flips) :]
    windows, count, features = parts[0].shape
    steps, batch, lags, columns = out_ref.shape
    per = columns // cw
    width = count // per
    rep = lax.axis_index("rep")
    for part, flip in zip(parts, flips):
        for w in range(windows):
            for g in range(per):
                first = pl.multiple_of(g * cw + (rep ^ flip) * width, width)
                right_ref[pl.ds(first, width), pl.ds(w * features, features)] = part[
                    w, pl.ds(g * width, width), :
                ]
    copies = []
    for i in range(steps):
        summed = lax.dot_general(
            left_ref[i * batch * lags : (i + 1) * batch * lags, :],
            right_ref[...],
            (((1,), (1,)), ((), ())),
            preferred_element_type=jnp.float32,
        )
        for n in range(batch):
            s = i * batch + n
            out_ref[i, n] = summed[n * lags : (n + 1) * lags] * scale_ref[s : s + 1, :]
        copies.append(
            pltpu.make_async_copy(
                out_ref.at[i], out_hbm.at[pl.ds(i * batch, batch)], sem.at[i]
            )
        )
        copies[-1].start()
    for copy in copies:
        copy.wait()


def correlate(parts, flips, left, scale, cw):
    quarter, columns = scale.shape
    steps = 8
    return pl.pallas_call(
        functools.partial(correlate_kernel, flips, cw),
        out_shape=jax.ShapeDtypeStruct((quarter, LAGS, columns), jnp.float32),
        in_specs=[VMEM] * (len(parts) + 2),
        out_specs=HBM,
        scratch_shapes=[
            pltpu.VMEM((columns, left.shape[1]), jnp.bfloat16),
            pltpu.VMEM((steps, quarter // steps, LAGS, columns), jnp.float32),
            pltpu.SemaphoreType.DMA((steps,)),
        ],
        compiler_params=pltpu.CompilerParams(vmem_limit_bytes=LIMIT),
        name="correlate",
    )(*parts, left, scale)


def swap(x, axis, flip):
    size = lax.axis_size(axis)
    return lax.ppermute(x, axis, [(i, i ^ flip) for i in range(size)])


def regroup(x):
    shards_in, rows, span = x.shape
    if span == CHUNK:
        return x
    joined = jnp.transpose(x, (1, 0, 2)).reshape(rows, -1, CHUNK)
    return jnp.transpose(joined, (1, 0, 2))


def gather_sources(low, high, prepare):
    chans, chan = lax.axis_size("chan"), lax.axis_index("chan")
    windows, quarter, span = low[0].shape
    flip = len(low)
    while flip:
        came = swap(high, "rep", flip)
        low = [part + came[n] for n, part in enumerate(low)]
        flip //= 2
        if flip:
            high = jnp.stack(low[flip:])
            low = low[:flip]
    mine = low[0]
    prepared = prepare(mine)
    held = mine.reshape(1, windows * quarter, span)
    if chans == 8 and span == CHUNK:
        pair = jnp.concatenate([held, swap(held, "chan", 1)], axis=0)
        pair, prepared = lax.optimization_barrier((pair, prepared))
        flips = (6, 4, 2)
        parts = [pair] + [swap(pair, "chan", flip) for flip in flips]
        return prepared, parts, tuple((flip, flip ^ 1) for flip in (0,) + flips)
    keys, flip = [0], 1
    while flip < chans:
        held = jnp.concatenate([held, swap(held, "chan", flip)], axis=0)
        keys = keys + [key ^ flip for key in keys]
        flip *= 2
    every = jnp.zeros_like(held).at[chan ^ jnp.asarray(keys, jnp.int32)].set(held)
    every = regroup(every)
    return prepared, (every,), ((None,) * every.shape[0],)


def shards(records, sources, dead_list):
    windows, groups, width, span = records.shape
    reps, chans = lax.axis_size("rep"), lax.axis_size("chan")
    cw = width * reps
    per = groups // chans
    blocks, *low, high = pack(records, sources, chans, reps)
    blocks = blocks.reshape(chans, windows * per * width, span)
    order = order_of(chans)
    arrived = lax.all_to_all(blocks, "chan", 0, 0, axis_index_groups=[list(order)], tiled=True)
    if span != CHUNK:
        arrived = regroup(jnp.stack([arrived[order.index(i)] for i in range(chans)]))
        order = tuple(range(arrived.shape[0]))
    table = jnp.asarray(dft_table(chans * span))

    def prepare(after):
        return stage(table, sources, dead_list, after, per, cw, width)

    (table, live, source_live, scale), parts, keys = gather_sources(low, high, prepare)
    tables = [table, jnp.asarray(sample_band()), jnp.asarray(bin_band())]
    spectra = channel_spectra(arrived, order, live, tables, windows)
    source_spec = source_spectra(parts, keys, source_live, tables)
    pieces, flips = [spectra], [0]
    flip = reps // 2
    while flip:
        others = [swap(piece, "rep", flip) for piece in pieces]
        pieces = pieces + others
        flips = flips + [f ^ flip for f in flips]
        flip //= 2
    left = lag_kernels(source_spec, windows)
    return correlate(pieces, flips, left, scale, cw)


def solution(mesh):
    placed = (P(None, None, "rep", "chan"), P(), P())
    return jax.shard_map(
        shards, mesh=mesh, in_specs=placed, out_specs=P("rep", None, "chan"), check_vma=False
    )
```

```python
import functools
import math

import jax
import jax.numpy as jnp
import numpy as np
from jax import lax
from jax.experimental import pallas as pl
from jax.experimental.pallas import tpu as pltpu
from jax.sharding import PartitionSpec as P

WINDOW_SAMPLES = 2048
K = 256
K0 = 16
HALF = 32
WH = 32
LAGS = 64
EPS = 1e-06

CHUNK = 256
EDGE = 128
ORDER = (3, 6, 1, 2, 7, 0, 5, 4)
VMEM = pl.BlockSpec(memory_space=pltpu.VMEM)
LIMIT = 16 * 1024 * 1024
STAGE_FLOPS = 1
HBM = pl.BlockSpec(memory_space=pltpu.HBM)


def dft_table(length):
    sample = np.arange(length, dtype=np.int64)[:, None]
    bin_index = K0 + np.arange(K, dtype=np.int64)[None, :]
    angle = (sample * bin_index % length) * (2.0 * math.pi / length)
    table = np.concatenate([np.cos(angle), -np.sin(angle)], axis=1)
    return table.astype(np.float32).astype(jnp.bfloat16)


def lag_tables():
    bin_index = K0 + np.arange(K, dtype=np.int64)[None, :]
    lag = np.arange(LAGS, dtype=np.int64)[:, None] - LAGS // 2
    angle = np.mod(lag * bin_index, WINDOW_SAMPLES) * (2.0 * math.pi / WINDOW_SAMPLES)
    return np.cos(angle).astype(np.float32), np.sin(angle).astype(np.float32)


def sample_band():
    source = np.arange(CHUNK + 2 * EDGE)[:, None] - EDGE
    target = np.arange(CHUNK)[None, :]
    return (np.abs(source - target) <= HALF).astype(np.float32).astype(jnp.bfloat16)


def bin_band():
    row = np.arange(K)[:, None]
    column = np.arange(K)[None, :]
    return (np.abs(row - column) <= WH).astype(np.float32).astype(jnp.bfloat16)


def order_of(chans):
    return ORDER if chans == len(ORDER) else tuple(range(chans))


def iota(shape, dim):
    return lax.broadcasted_iota(jnp.int32, shape, dim)


def columns_of(row):
    return jnp.concatenate(
        [
            jnp.broadcast_to(row[:, i : i + 128], (128, 128)).T
            for i in range(0, row.shape[1], 128)
        ],
        axis=0,
    )


def listed(ids, dead):
    hit = jnp.zeros((ids.shape[0], 128), jnp.float32)
    for i in range(0, dead.shape[1], 128):
        hit = jnp.maximum(hit, jnp.where(ids == dead[:, i : i + 128], 1.0, 0.0))
    return jnp.max(hit, axis=1, keepdims=True)


def pack_kernel(cw, rec_hbm, src_hbm, out_hbm, *refs):
    *low_refs, high_ref, out_ref, src_ref, pick_ref, sem = refs
    windows, groups, width, span = rec_hbm.shape
    per = groups // out_ref.shape[0]
    order = order_of(out_ref.shape[0])
    brought = pltpu.make_async_copy(src_hbm, src_ref, sem.at[windows, 0])
    brought.start()
    copies = []
    for w in range(windows):
        copies.append(
            [
                pltpu.make_async_copy(
                    rec_hbm.at[w, pl.ds(member * per, per)], out_ref.at[n, w], sem.at[w, n]
                )
                for n, member in enumerate(order)
            ]
        )
        for copy in copies[-1]:
            copy.start()
    reps = cw // width
    rep = lax.axis_index("rep")
    count = src_ref.shape[1]
    quarter = count // reps
    local = groups * width
    place = iota((count, local), 1)
    ids = (place // width) * cw + rep * width + place % width
    brought.wait()
    wide = jnp.concatenate([columns_of(src_ref[...])] * (local // 128), axis=1)
    onehot = jnp.where(wide == ids, 1.0, 0.0).astype(jnp.bfloat16)
    sent = []
    for w in range(windows):
        for n in range(len(order)):
            copies[w][n].wait()
            sent.append(
                pltpu.make_async_copy(out_ref.at[n, w], out_hbm.at[n, w], sem.at[windows + 1 + w, n])
            )
            sent[-1].start()
    for w in range(windows):
        rows = jnp.concatenate(
            [out_ref[order.index(g // per), w, g % per] for g in range(groups)], axis=0
        )
        pick_ref[...] = jnp.dot(onehot, rows, preferred_element_type=jnp.float32)
        for flip in range(reps):
            first = pl.multiple_of((rep ^ flip) * quarter, quarter)
            picked = pick_ref[pl.ds(first, quarter), :].astype(jnp.bfloat16)
            if flip < reps // 2:
                low_refs[flip][w] = picked
            else:
                high_ref[flip - reps // 2, w] = picked
    for copy in sent:
        copy.wait()


def in_hbm(*arrays):
    return [pltpu.with_memory_space_constraint(array, pltpu.HBM) for array in arrays]


def pack(records, sources, chans, reps):
    windows, groups, width, span = records.shape
    count = sources.shape[0]
    per = groups // chans
    part = (windows, count // reps, span)
    return pl.pallas_call(
        functools.partial(pack_kernel, width * reps),
        out_shape=(
            jax.ShapeDtypeStruct((chans, windows, per, width, span), jnp.bfloat16),
            *[jax.ShapeDtypeStruct(part, jnp.bfloat16)] * (reps // 2),
            jax.ShapeDtypeStruct((reps // 2,) + part, jnp.bfloat16),
        ),
        in_specs=[HBM] * 2,
        out_specs=(HBM,) + (VMEM,) * (reps // 2 + 1),
        scratch_shapes=[
            pltpu.VMEM((chans, windows, per, width, span), jnp.bfloat16),
            pltpu.VMEM((1, count), jnp.int32),
            pltpu.VMEM((count, span), jnp.float32),
            pltpu.SemaphoreType.DMA((1 + 2 * windows, chans)),
        ],
        compiler_params=pltpu.CompilerParams(vmem_limit_bytes=LIMIT),
        name="pack",
    )(*in_hbm(records, sources.reshape(1, count)))


def stage_kernel(
    cw, width, table_hbm, src_hbm, dead_hbm, after_hbm,
    table_ref, live_ref, source_live_ref, scale_ref,
    src_ref, dead_ref, pick_ref, sem,
):
    copies = [
        pltpu.make_async_copy(src_hbm, src_ref, sem.at[0]),
        pltpu.make_async_copy(dead_hbm, dead_ref, sem.at[1]),
        pltpu.make_async_copy(table_hbm, table_ref, sem.at[2]),
    ]
    for copy in copies:
        copy.start()
    windows = dead_ref.shape[0]
    rep, chan = lax.axis_index("rep"), lax.axis_index("chan")
    count = src_ref.shape[1]
    quarter, columns = scale_ref.shape
    per = columns // cw
    here = pl.ds(pl.multiple_of(rep * quarter, quarter), quarter)
    row = iota((per * width, 1), 0)
    row_ids = (chan * per + row // width) * cw + rep * width + row % width
    block_ids = chan * columns + iota((1, columns), 1)
    copies[0].wait()
    copies[1].wait()
    column = columns_of(src_ref[...])
    pick_ref[...] = column
    mine = pick_ref[here, :]
    pairs = jnp.zeros((quarter, columns), jnp.float32)
    for w in range(windows):
        dead = dead_ref[w : w + 1, :]
        live_ref[w * per * width : (w + 1) * per * width, :] = 1.0 - listed(row_ids, dead)
        source_live = 1.0 - listed(mine, dead)
        source_live_ref[w * quarter : (w + 1) * quarter, :] = source_live
        dead_column = columns_of(dead)
        hits = [
            jnp.max(
                jnp.where(dead_column == block_ids[:, i : i + 128], 1.0, 0.0), axis=0, keepdims=True
            )
            for i in range(0, columns, 128)
        ]
        pairs += source_live * (1.0 - jnp.concatenate(hits, axis=1))
    scale_ref[...] = 1.0 / (math.sqrt(K) * jnp.maximum(pairs, 1.0))
    copies[2].wait()


def stage(table, sources, dead_list, after, per, cw, width):
    windows = dead_list.shape[0]
    count = sources.shape[0]
    quarter = count // (cw // width)
    return pl.pallas_call(
        functools.partial(stage_kernel, cw, width),
        out_shape=(
            jax.ShapeDtypeStruct(table.shape, table.dtype),
            jax.ShapeDtypeStruct((windows * per * width, 1), jnp.float32),
            jax.ShapeDtypeStruct((windows * quarter, 1), jnp.float32),
            jax.ShapeDtypeStruct((quarter, per * cw), jnp.float32),
        ),
        in_specs=[HBM] * 3 + [pl.BlockSpec(memory_space=pl.ANY)],
        out_specs=(VMEM,) * 4,
        scratch_shapes=[
            pltpu.VMEM((1, count), jnp.int32),
            pltpu.VMEM(dead_list.shape, jnp.int32),
            pltpu.VMEM((count, 128), jnp.int32),
            pltpu.SemaphoreType.DMA((3,)),
        ],
        compiler_params=pltpu.CompilerParams(vmem_limit_bytes=LIMIT),
        cost_estimate=pl.CostEstimate(
            flops=STAGE_FLOPS, bytes_accessed=4 << 20, transcendentals=0
        ),
        name="stage",
    )(*in_hbm(table, sources.reshape(1, count), dead_list), after)


def whiten_rows(x_ref, order, ext_ref, table_ref, band_ref, bins_ref):
    pieces, rows, _ = x_ref.shape
    x = [x_ref.at[order.index(i)] for i in range(pieces)]
    length = pieces * CHUNK
    for i in range(pieces):
        here = pl.ds(i * rows, rows)
        ext_ref[here, EDGE : EDGE + CHUNK] = jnp.abs(x[i][...])
        blank = jnp.zeros((rows, EDGE), jnp.bfloat16)
        ext_ref[here, :EDGE] = jnp.abs(x[i - 1][:, CHUNK - EDGE :]) if i else blank
        ext_ref[here, EDGE + CHUNK :] = (
            jnp.abs(x[i + 1][:, :EDGE]) if i < pieces - 1 else blank
        )
    totals = jnp.dot(ext_ref[...], band_ref[...], preferred_element_type=jnp.float32)
    chunks = []
    for i in range(pieces):
        sample = iota((1, CHUNK), 1) + i * CHUNK
        counts = jnp.minimum(sample, HALF) + jnp.minimum(length - 1 - sample, HALF) + 1
        mean = totals[i * rows : (i + 1) * rows] * (1.0 / counts.astype(jnp.float32))
        normed = (x[i][...].astype(jnp.float32) / (mean + EPS)).astype(jnp.bfloat16)
        chunks.append(normed)
    spectrum = jnp.dot(
        jnp.concatenate(chunks, axis=1), table_ref[...], preferred_element_type=jnp.float32
    )
    real_part, imag_part = spectrum[:, :K], spectrum[:, K:]
    amplitude = jnp.sqrt(real_part * real_part + imag_part * imag_part)
    high = amplitude.astype(jnp.bfloat16)
    rest = amplitude - high.astype(jnp.float32)
    middle = rest.astype(jnp.bfloat16)
    low = (rest - middle.astype(jnp.float32)).astype(jnp.bfloat16)
    stacked = jnp.concatenate([high, middle, low], axis=0)
    sums = jnp.dot(stacked, bins_ref[...], preferred_element_type=jnp.float32)
    place = iota((1, K), 1)
    width = jnp.minimum(place, WH) + jnp.minimum(K - 1 - place, WH) + 1
    smooth = (sums[:rows] + sums[rows : 2 * rows] + sums[2 * rows :]) * (
        1.0 / width.astype(jnp.float32)
    )
    scale = 1.0 / (smooth + EPS)
    return real_part * scale, imag_part * scale


def channel_kernel(order, x_ref, live_ref, table_ref, band_ref, bins_ref, out_ref, ext_ref):
    windows, count, _ = out_ref.shape
    real_part, imag_part = whiten_rows(x_ref, order, ext_ref, table_ref, band_ref, bins_ref)
    for w in range(windows):
        here = slice(w * count, (w + 1) * count)
        out_ref[w, :, :K] = (real_part[here] * live_ref[here, :]).astype(jnp.bfloat16)
        out_ref[w, :, K:] = (imag_part[here] * live_ref[here, :]).astype(jnp.bfloat16)


def channel_spectra(x, order, live, tables, windows):
    pieces, rows, _ = x.shape
    return pl.pallas_call(
        functools.partial(channel_kernel, order),
        out_shape=jax.ShapeDtypeStruct((windows, rows // windows, 2 * K), jnp.bfloat16),
        in_specs=[VMEM] * 5,
        out_specs=VMEM,
        scratch_shapes=[pltpu.VMEM((pieces * rows, CHUNK + 2 * EDGE), jnp.bfloat16)],
        compiler_params=pltpu.CompilerParams(vmem_limit_bytes=LIMIT),
        cost_estimate=pl.CostEstimate(
            flops=1, bytes_accessed=1, transcendentals=0
        ),
        name="channel_spectra",
    )(x, live, *tables)


def source_kernel(keys, *refs):
    parts = refs[: len(keys)]
    live_ref, table_ref, band_ref, bins_ref = refs[len(keys) : -3]
    out_ref, x_ref, ext_ref = refs[-3:]
    chan = lax.axis_index("chan")
    for part, slots in zip(parts, keys):
        for n, key in enumerate(slots):
            x_ref[chan ^ key if key is not None else n] = part[n]
    order = tuple(range(x_ref.shape[0]))
    real_part, imag_part = whiten_rows(x_ref, order, ext_ref, table_ref, band_ref, bins_ref)
    out_ref[:, :K] = (real_part * live_ref[...]).astype(jnp.bfloat16)
    out_ref[:, K:] = (imag_part * live_ref[...]).astype(jnp.bfloat16)


def source_spectra(parts, keys, live, tables):
    rows = parts[0].shape[1]
    pieces = sum(len(slots) for slots in keys)
    return pl.pallas_call(
        functools.partial(source_kernel, keys),
        out_shape=jax.ShapeDtypeStruct((rows, 2 * K), jnp.bfloat16),
        in_specs=[VMEM] * (len(parts) + 4),
        out_specs=VMEM,
        scratch_shapes=[
            pltpu.VMEM((pieces, rows, CHUNK), jnp.bfloat16),
            pltpu.VMEM((pieces * rows, CHUNK + 2 * EDGE), jnp.bfloat16),
        ],
        compiler_params=pltpu.CompilerParams(vmem_limit_bytes=LIMIT),
        cost_estimate=pl.CostEstimate(flops=1 << 34, bytes_accessed=8 << 20, transcendentals=0),
        name="source_spectra",
    )(*parts, live, *tables)


def lag_kernel(windows, spec_ref, cos_ref, sin_ref, out_ref):
    spec = spec_ref[...].astype(jnp.float32)
    quarter = spec.shape[0] // windows
    lags = cos_ref.shape[0]
    for s in range(quarter):
        for w in range(windows):
            u = spec[w * quarter + s : w * quarter + s + 1, :K]
            v = spec[w * quarter + s : w * quarter + s + 1, K:]
            rows = slice(s * lags, (s + 1) * lags)
            first = w * 2 * K
            out_ref[rows, first : first + K] = (
                u * cos_ref[...] + v * sin_ref[...]
            ).astype(jnp.bfloat16)
            out_ref[rows, first + K : first + 2 * K] = (
                v * cos_ref[...] - u * sin_ref[...]
            ).astype(jnp.bfloat16)


def lag_kernels(spec, windows):
    rows = spec.shape[0]
    cosine, sine = lag_tables()
    return pl.pallas_call(
        functools.partial(lag_kernel, windows),
        out_shape=jax.ShapeDtypeStruct((rows // windows * LAGS, windows * 2 * K), jnp.bfloat16),
        in_specs=[VMEM] * 3,
        out_specs=VMEM,
        compiler_params=pltpu.CompilerParams(vmem_limit_bytes=LIMIT),
        cost_estimate=pl.CostEstimate(flops=1 << 34, bytes_accessed=8 << 20, transcendentals=0),
        name="lag_kernels",
    )(spec, jnp.asarray(cosine), jnp.asarray(sine))


def correlate_kernel(flips, cw, *refs):
    parts = refs[: len(flips)]
    left_ref, scale_ref, out_hbm, right_ref, out_ref, sem = refs[len(flips) :]
    windows, count, features = parts[0].shape
    steps, batch, lags, columns = out_ref.shape
    per = columns // cw
    width = count // per
    rep = lax.axis_index("rep")
    for part, flip in zip(parts, flips):
        for w in range(windows):
            for g in range(per):
                first = pl.multiple_of(g * cw + (rep ^ flip) * width, width)
                right_ref[pl.ds(first, width), pl.ds(w * features, features)] = part[
                    w, pl.ds(g * width, width), :
                ]
    copies = []
    for i in range(steps):
        summed = lax.dot_general(
            left_ref[i * batch * lags : (i + 1) * batch * lags, :],
            right_ref[...],
            (((1,), (1,)), ((), ())),
            preferred_element_type=jnp.float32,
        )
        for n in range(batch):
            s = i * batch + n
            out_ref[i, n] = summed[n * lags : (n + 1) * lags] * scale_ref[s : s + 1, :]
        copies.append(
            pltpu.make_async_copy(
                out_ref.at[i], out_hbm.at[pl.ds(i * batch, batch)], sem.at[i]
            )
        )
        copies[-1].start()
    for copy in copies:
        copy.wait()


def correlate(parts, flips, left, scale, cw):
    quarter, columns = scale.shape
    steps = 8
    return pl.pallas_call(
        functools.partial(correlate_kernel, flips, cw),
        out_shape=jax.ShapeDtypeStruct((quarter, LAGS, columns), jnp.float32),
        in_specs=[VMEM] * (len(parts) + 2),
        out_specs=HBM,
        scratch_shapes=[
            pltpu.VMEM((columns, left.shape[1]), jnp.bfloat16),
            pltpu.VMEM((steps, quarter // steps, LAGS, columns), jnp.float32),
            pltpu.SemaphoreType.DMA((steps,)),
        ],
        compiler_params=pltpu.CompilerParams(vmem_limit_bytes=LIMIT),
        name="correlate",
    )(*parts, left, scale)


def swap(x, axis, flip):
    size = lax.axis_size(axis)
    return lax.ppermute(x, axis, [(i, i ^ flip) for i in range(size)])


def regroup(x):
    shards_in, rows, span = x.shape
    if span == CHUNK:
        return x
    joined = jnp.transpose(x, (1, 0, 2)).reshape(rows, -1, CHUNK)
    return jnp.transpose(joined, (1, 0, 2))


def gather_sources(low, high, prepare):
    chans, chan = lax.axis_size("chan"), lax.axis_index("chan")
    windows, quarter, span = low[0].shape
    given = list(low) + [high[n] for n in range(len(low))]
    mine = given[0]
    for flip in range(1, len(given)):
        mine = mine + swap(given[flip], "rep", flip)
    prepared = prepare(mine)
    held = mine.reshape(1, windows * quarter, span)
    if chans == 8 and span == CHUNK:
        pair = jnp.concatenate([held, swap(held, "chan", 1)], axis=0)
        pair, prepared = lax.optimization_barrier((pair, prepared))
        flips = (6, 4, 2)
        parts = [pair] + [swap(pair, "chan", flip) for flip in flips]
        return prepared, parts, tuple((flip, flip ^ 1) for flip in (0,) + flips)
    keys, flip = [0], 1
    while flip < chans:
        held = jnp.concatenate([held, swap(held, "chan", flip)], axis=0)
        keys = keys + [key ^ flip for key in keys]
        flip *= 2
    every = jnp.zeros_like(held).at[chan ^ jnp.asarray(keys, jnp.int32)].set(held)
    every = regroup(every)
    return prepared, (every,), ((None,) * every.shape[0],)


def shards(records, sources, dead_list):
    windows, groups, width, span = records.shape
    reps, chans = lax.axis_size("rep"), lax.axis_size("chan")
    cw = width * reps
    per = groups // chans
    blocks, *low, high = pack(records, sources, chans, reps)
    blocks = blocks.reshape(chans, windows * per * width, span)
    order = order_of(chans)
    arrived = lax.all_to_all(blocks, "chan", 0, 0, axis_index_groups=[list(order)], tiled=True)
    if span != CHUNK:
        arrived = regroup(jnp.stack([arrived[order.index(i)] for i in range(chans)]))
        order = tuple(range(arrived.shape[0]))
    table = jnp.asarray(dft_table(chans * span))

    def prepare(after):
        return stage(table, sources, dead_list, after, per, cw, width)

    (table, live, source_live, scale), parts, keys = gather_sources(low, high, prepare)
    tables = [table, jnp.asarray(sample_band()), jnp.asarray(bin_band())]
    spectra = channel_spectra(arrived, order, live, tables, windows)
    source_spec = source_spectra(parts, keys, source_live, tables)
    pieces, flips = [spectra], [0]
    flip = reps // 2
    while flip:
        others = [swap(piece, "rep", flip) for piece in pieces]
        pieces = pieces + others
        flips = flips + [f ^ flip for f in flips]
        flip //= 2
    left = lag_kernels(source_spec, windows)
    return correlate(pieces, flips, left, scale, cw)


def solution(mesh):
    placed = (P(None, None, "rep", "chan"), P(), P())
    return jax.shard_map(
        shards, mesh=mesh, in_specs=placed, out_specs=P("rep", None, "chan"), check_vma=False
    )
```

```python
import functools
import math

import jax
import jax.numpy as jnp
import numpy as np
from jax import lax
from jax.experimental import pallas as pl
from jax.experimental.pallas import tpu as pltpu
from jax.sharding import PartitionSpec as P

WINDOW_SAMPLES = 2048
K = 256
K0 = 16
HALF = 32
WH = 32
LAGS = 64
EPS = 1e-06

CHUNK = 256
EDGE = 128
ORDER = (3, 6, 1, 2, 7, 0, 5, 4)
VMEM = pl.BlockSpec(memory_space=pltpu.VMEM)
LIMIT = 16 * 1024 * 1024
STAGE_FLOPS = 1
HBM = pl.BlockSpec(memory_space=pltpu.HBM)


def dft_table(length):
    sample = np.arange(length, dtype=np.int64)[:, None]
    bin_index = K0 + np.arange(K, dtype=np.int64)[None, :]
    angle = (sample * bin_index % length) * (2.0 * math.pi / length)
    table = np.concatenate([np.cos(angle), -np.sin(angle)], axis=1)
    return table.astype(np.float32).astype(jnp.bfloat16)


def lag_tables():
    bin_index = K0 + np.arange(K, dtype=np.int64)[None, :]
    lag = np.arange(LAGS, dtype=np.int64)[:, None] - LAGS // 2
    angle = np.mod(lag * bin_index, WINDOW_SAMPLES) * (2.0 * math.pi / WINDOW_SAMPLES)
    return np.cos(angle).astype(np.float32), np.sin(angle).astype(np.float32)


def sample_band():
    source = np.arange(CHUNK + 2 * EDGE)[:, None] - EDGE
    target = np.arange(CHUNK)[None, :]
    return (np.abs(source - target) <= HALF).astype(np.float32).astype(jnp.bfloat16)


def bin_band():
    row = np.arange(K)[:, None]
    column = np.arange(K)[None, :]
    return (np.abs(row - column) <= WH).astype(np.float32).astype(jnp.bfloat16)


def order_of(chans):
    return ORDER if chans == len(ORDER) else tuple(range(chans))


def iota(shape, dim):
    return lax.broadcasted_iota(jnp.int32, shape, dim)


def columns_of(row):
    return jnp.concatenate(
        [
            jnp.broadcast_to(row[:, i : i + 128], (128, 128)).T
            for i in range(0, row.shape[1], 128)
        ],
        axis=0,
    )


def listed(ids, dead):
    hit = jnp.zeros((ids.shape[0], 128), jnp.float32)
    for i in range(0, dead.shape[1], 128):
        hit = jnp.maximum(hit, jnp.where(ids == dead[:, i : i + 128], 1.0, 0.0))
    return jnp.max(hit, axis=1, keepdims=True)


def pack_kernel(cw, rec_hbm, src_hbm, out_hbm, *refs):
    *low_refs, high_ref, out_ref, src_ref, pick_ref, sem = refs
    windows, groups, width, span = rec_hbm.shape
    per = groups // out_ref.shape[0]
    order = order_of(out_ref.shape[0])
    brought = pltpu.make_async_copy(src_hbm, src_ref, sem.at[windows, 0])
    brought.start()
    copies = []
    for w in range(windows):
        copies.append(
            [
                pltpu.make_async_copy(
                    rec_hbm.at[w, pl.ds(member * per, per)], out_ref.at[n, w], sem.at[w, n]
                )
                for n, member in enumerate(order)
            ]
        )
        for copy in copies[-1]:
            copy.start()
    reps = cw // width
    rep = lax.axis_index("rep")
    count = src_ref.shape[1]
    quarter = count // reps
    local = groups * width
    place = iota((count, local), 1)
    ids = (place // width) * cw + rep * width + place % width
    brought.wait()
    wide = jnp.concatenate([columns_of(src_ref[...])] * (local // 128), axis=1)
    onehot = jnp.where(wide == ids, 1.0, 0.0).astype(jnp.bfloat16)
    sent = []
    for w in range(windows):
        for n in range(len(order)):
            copies[w][n].wait()
            sent.append(
                pltpu.make_async_copy(out_ref.at[n, w], out_hbm.at[n, w], sem.at[windows + 1 + w, n])
            )
            sent[-1].start()
    for w in range(windows):
        rows = jnp.concatenate(
            [out_ref[order.index(g // per), w, g % per] for g in range(groups)], axis=0
        )
        pick_ref[...] = jnp.dot(onehot, rows, preferred_element_type=jnp.float32)
        for flip in range(reps):
            first = pl.multiple_of((rep ^ flip) * quarter, quarter)
            picked = pick_ref[pl.ds(first, quarter), :].astype(jnp.bfloat16)
            if flip < reps // 2:
                low_refs[flip][w] = picked
            else:
                high_ref[flip - reps // 2, w] = picked
    for copy in sent:
        copy.wait()


def in_hbm(*arrays):
    return [pltpu.with_memory_space_constraint(array, pltpu.HBM) for array in arrays]


def pack(records, sources, chans, reps):
    windows, groups, width, span = records.shape
    count = sources.shape[0]
    per = groups // chans
    part = (windows, count // reps, span)
    return pl.pallas_call(
        functools.partial(pack_kernel, width * reps),
        out_shape=(
            jax.ShapeDtypeStruct((chans, windows, per, width, span), jnp.bfloat16),
            *[jax.ShapeDtypeStruct(part, jnp.bfloat16)] * (reps // 2),
            jax.ShapeDtypeStruct((reps // 2,) + part, jnp.bfloat16),
        ),
        in_specs=[HBM] * 2,
        out_specs=(HBM,) + (VMEM,) * (reps // 2 + 1),
        scratch_shapes=[
            pltpu.VMEM((chans, windows, per, width, span), jnp.bfloat16),
            pltpu.VMEM((1, count), jnp.int32),
            pltpu.VMEM((count, span), jnp.float32),
            pltpu.SemaphoreType.DMA((1 + 2 * windows, chans)),
        ],
        compiler_params=pltpu.CompilerParams(vmem_limit_bytes=LIMIT),
        name="pack",
    )(*in_hbm(records, sources.reshape(1, count)))


def stage_kernel(
    cw, width, table_hbm, src_hbm, dead_hbm, after_hbm,
    table_ref, live_ref, source_live_ref, scale_ref,
    src_ref, dead_ref, pick_ref, sem,
):
    copies = [
        pltpu.make_async_copy(src_hbm, src_ref, sem.at[0]),
        pltpu.make_async_copy(dead_hbm, dead_ref, sem.at[1]),
        pltpu.make_async_copy(table_hbm, table_ref, sem.at[2]),
    ]
    for copy in copies:
        copy.start()
    windows = dead_ref.shape[0]
    rep, chan = lax.axis_index("rep"), lax.axis_index("chan")
    count = src_ref.shape[1]
    quarter, columns = scale_ref.shape
    per = columns // cw
    here = pl.ds(pl.multiple_of(rep * quarter, quarter), quarter)
    row = iota((per * width, 1), 0)
    row_ids = (chan * per + row // width) * cw + rep * width + row % width
    block_ids = chan * columns + iota((1, columns), 1)
    copies[0].wait()
    copies[1].wait()
    column = columns_of(src_ref[...])
    pick_ref[...] = column
    mine = pick_ref[here, :]
    pairs = jnp.zeros((quarter, columns), jnp.float32)
    for w in range(windows):
        dead = dead_ref[w : w + 1, :]
        live_ref[w * per * width : (w + 1) * per * width, :] = 1.0 - listed(row_ids, dead)
        source_live = 1.0 - listed(mine, dead)
        source_live_ref[w * quarter : (w + 1) * quarter, :] = source_live
        dead_column = columns_of(dead)
        hits = [
            jnp.max(
                jnp.where(dead_column == block_ids[:, i : i + 128], 1.0, 0.0), axis=0, keepdims=True
            )
            for i in range(0, columns, 128)
        ]
        pairs += source_live * (1.0 - jnp.concatenate(hits, axis=1))
    scale_ref[...] = 1.0 / (math.sqrt(K) * jnp.maximum(pairs, 1.0))
    copies[2].wait()


def stage(table, sources, dead_list, after, per, cw, width):
    windows = dead_list.shape[0]
    count = sources.shape[0]
    quarter = count // (cw // width)
    return pl.pallas_call(
        functools.partial(stage_kernel, cw, width),
        out_shape=(
            jax.ShapeDtypeStruct(table.shape, table.dtype),
            jax.ShapeDtypeStruct((windows * per * width, 1), jnp.float32),
            jax.ShapeDtypeStruct((windows * quarter, 1), jnp.float32),
            jax.ShapeDtypeStruct((quarter, per * cw), jnp.float32),
        ),
        in_specs=[HBM] * 3 + [pl.BlockSpec(memory_space=pl.ANY)],
        out_specs=(VMEM,) * 4,
        scratch_shapes=[
            pltpu.VMEM((1, count), jnp.int32),
            pltpu.VMEM(dead_list.shape, jnp.int32),
            pltpu.VMEM((count, 128), jnp.int32),
            pltpu.SemaphoreType.DMA((3,)),
        ],
        compiler_params=pltpu.CompilerParams(vmem_limit_bytes=LIMIT),
        cost_estimate=pl.CostEstimate(
            flops=STAGE_FLOPS, bytes_accessed=4 << 20, transcendentals=0
        ),
        name="stage",
    )(*in_hbm(table, sources.reshape(1, count), dead_list), after)


def whiten_rows(x_ref, order, group, table_ref, band_ref, bins_ref):
    pieces, rows, _ = x_ref.shape
    x = [x_ref.at[order.index(i)] for i in range(pieces)]
    length = pieces * CHUNK
    views, chunks = [], []
    blank = jnp.zeros((rows, EDGE), jnp.bfloat16)
    for i in range(pieces):
        before = jnp.abs(x[i - 1][:, CHUNK - EDGE :]) if i else blank
        after = jnp.abs(x[i + 1][:, :EDGE]) if i < pieces - 1 else blank
        views.append(jnp.concatenate([before, jnp.abs(x[i][...]), after], axis=1))
    for i in range(pieces):
        n = i % group
        if n == 0:
            view = jnp.concatenate(views[i : i + group], axis=0)
            totals = jnp.dot(view, band_ref[...], preferred_element_type=jnp.float32)
        sample = iota((1, CHUNK), 1) + i * CHUNK
        counts = jnp.minimum(sample, HALF) + jnp.minimum(length - 1 - sample, HALF) + 1
        mean = totals[n * rows : (n + 1) * rows] * (1.0 / counts.astype(jnp.float32))
        chunks.append((x[i][...].astype(jnp.float32) / (mean + EPS)).astype(jnp.bfloat16))
    spectrum = jnp.dot(
        jnp.concatenate(chunks, axis=1), table_ref[...], preferred_element_type=jnp.float32
    )
    real_part, imag_part = spectrum[:, :K], spectrum[:, K:]
    amplitude = jnp.sqrt(real_part * real_part + imag_part * imag_part)
    high = amplitude.astype(jnp.bfloat16)
    rest = amplitude - high.astype(jnp.float32)
    middle = rest.astype(jnp.bfloat16)
    low = (rest - middle.astype(jnp.float32)).astype(jnp.bfloat16)
    stacked = jnp.concatenate([high, middle, low], axis=0)
    sums = jnp.dot(stacked, bins_ref[...], preferred_element_type=jnp.float32)
    place = iota((1, K), 1)
    width = jnp.minimum(place, WH) + jnp.minimum(K - 1 - place, WH) + 1
    smooth = (sums[:rows] + sums[rows : 2 * rows] + sums[2 * rows :]) * (
        1.0 / width.astype(jnp.float32)
    )
    scale = 1.0 / (smooth + EPS)
    return real_part * scale, imag_part * scale


def channel_kernel(order, x_ref, live_ref, table_ref, band_ref, bins_ref, out_ref):
    windows, count, _ = out_ref.shape
    real_part, imag_part = whiten_rows(x_ref, order, 1, table_ref, band_ref, bins_ref)
    for w in range(windows):
        here = slice(w * count, (w + 1) * count)
        out_ref[w, :, :K] = (real_part[here] * live_ref[here, :]).astype(jnp.bfloat16)
        out_ref[w, :, K:] = (imag_part[here] * live_ref[here, :]).astype(jnp.bfloat16)


def channel_spectra(x, order, live, tables, windows):
    pieces, rows, _ = x.shape
    return pl.pallas_call(
        functools.partial(channel_kernel, order),
        out_shape=jax.ShapeDtypeStruct((windows, rows // windows, 2 * K), jnp.bfloat16),
        in_specs=[VMEM] * 5,
        out_specs=VMEM,
        compiler_params=pltpu.CompilerParams(vmem_limit_bytes=LIMIT),
        cost_estimate=pl.CostEstimate(
            flops=1, bytes_accessed=1, transcendentals=0
        ),
        name="channel_spectra",
    )(x, live, *tables)


def source_kernel(keys, *refs):
    parts = refs[: len(keys)]
    live_ref, table_ref, band_ref, bins_ref = refs[len(keys) : -2]
    out_ref, x_ref = refs[-2:]
    chan = lax.axis_index("chan")
    for part, slots in zip(parts, keys):
        for n, key in enumerate(slots):
            x_ref[chan ^ key if key is not None else n] = part[n]
    order = tuple(range(x_ref.shape[0]))
    real_part, imag_part = whiten_rows(x_ref, order, len(order), table_ref, band_ref, bins_ref)
    out_ref[:, :K] = (real_part * live_ref[...]).astype(jnp.bfloat16)
    out_ref[:, K:] = (imag_part * live_ref[...]).astype(jnp.bfloat16)


def source_spectra(parts, keys, live, tables):
    rows = parts[0].shape[1]
    pieces = sum(len(slots) for slots in keys)
    return pl.pallas_call(
        functools.partial(source_kernel, keys),
        out_shape=jax.ShapeDtypeStruct((rows, 2 * K), jnp.bfloat16),
        in_specs=[VMEM] * (len(parts) + 4),
        out_specs=VMEM,
        scratch_shapes=[
            pltpu.VMEM((pieces, rows, CHUNK), jnp.bfloat16),
        ],
        compiler_params=pltpu.CompilerParams(vmem_limit_bytes=LIMIT),
        cost_estimate=pl.CostEstimate(flops=1 << 34, bytes_accessed=8 << 20, transcendentals=0),
        name="source_spectra",
    )(*parts, live, *tables)


def lag_kernel(windows, spec_ref, cos_ref, sin_ref, out_ref):
    spec = spec_ref[...].astype(jnp.float32)
    quarter = spec.shape[0] // windows
    lags = cos_ref.shape[0]
    for s in range(quarter):
        for w in range(windows):
            u = spec[w * quarter + s : w * quarter + s + 1, :K]
            v = spec[w * quarter + s : w * quarter + s + 1, K:]
            rows = slice(s * lags, (s + 1) * lags)
            first = w * 2 * K
            out_ref[rows, first : first + K] = (
                u * cos_ref[...] + v * sin_ref[...]
            ).astype(jnp.bfloat16)
            out_ref[rows, first + K : first + 2 * K] = (
                v * cos_ref[...] - u * sin_ref[...]
            ).astype(jnp.bfloat16)


def lag_kernels(spec, windows):
    rows = spec.shape[0]
    cosine, sine = lag_tables()
    return pl.pallas_call(
        functools.partial(lag_kernel, windows),
        out_shape=jax.ShapeDtypeStruct((rows // windows * LAGS, windows * 2 * K), jnp.bfloat16),
        in_specs=[VMEM] * 3,
        out_specs=VMEM,
        compiler_params=pltpu.CompilerParams(vmem_limit_bytes=LIMIT),
        cost_estimate=pl.CostEstimate(flops=1 << 34, bytes_accessed=8 << 20, transcendentals=0),
        name="lag_kernels",
    )(spec, jnp.asarray(cosine), jnp.asarray(sine))


def correlate_kernel(flips, cw, *refs):
    parts = refs[: len(flips)]
    left_ref, scale_ref, out_hbm, right_ref, out_ref, sem = refs[len(flips) :]
    windows, count, features = parts[0].shape
    steps, batch, lags, columns = out_ref.shape
    per = columns // cw
    width = count // per
    rep = lax.axis_index("rep")
    for part, flip in zip(parts, flips):
        for w in range(windows):
            for g in range(per):
                first = pl.multiple_of(g * cw + (rep ^ flip) * width, width)
                right_ref[pl.ds(first, width), pl.ds(w * features, features)] = part[
                    w, pl.ds(g * width, width), :
                ]
    copies = []
    for i in range(steps):
        summed = lax.dot_general(
            left_ref[i * batch * lags : (i + 1) * batch * lags, :],
            right_ref[...],
            (((1,), (1,)), ((), ())),
            preferred_element_type=jnp.float32,
        )
        for n in range(batch):
            s = i * batch + n
            out_ref[i, n] = summed[n * lags : (n + 1) * lags] * scale_ref[s : s + 1, :]
        copies.append(
            pltpu.make_async_copy(
                out_ref.at[i], out_hbm.at[pl.ds(i * batch, batch)], sem.at[i]
            )
        )
        copies[-1].start()
    for copy in copies:
        copy.wait()


def correlate(parts, flips, left, scale, cw):
    quarter, columns = scale.shape
    steps = 8
    return pl.pallas_call(
        functools.partial(correlate_kernel, flips, cw),
        out_shape=jax.ShapeDtypeStruct((quarter, LAGS, columns), jnp.float32),
        in_specs=[VMEM] * (len(parts) + 2),
        out_specs=HBM,
        scratch_shapes=[
            pltpu.VMEM((columns, left.shape[1]), jnp.bfloat16),
            pltpu.VMEM((steps, quarter // steps, LAGS, columns), jnp.float32),
            pltpu.SemaphoreType.DMA((steps,)),
        ],
        compiler_params=pltpu.CompilerParams(vmem_limit_bytes=LIMIT),
        name="correlate",
    )(*parts, left, scale)


def swap(x, axis, flip):
    size = lax.axis_size(axis)
    return lax.ppermute(x, axis, [(i, i ^ flip) for i in range(size)])


def regroup(x):
    shards_in, rows, span = x.shape
    if span == CHUNK:
        return x
    joined = jnp.transpose(x, (1, 0, 2)).reshape(rows, -1, CHUNK)
    return jnp.transpose(joined, (1, 0, 2))


def gather_sources(low, high, prepare):
    chans, chan = lax.axis_size("chan"), lax.axis_index("chan")
    windows, quarter, span = low[0].shape
    given = list(low) + [high[n] for n in range(len(low))]
    mine = given[0]
    for flip in range(1, len(given)):
        mine = mine + swap(given[flip], "rep", flip)
    prepared = prepare(mine)
    held = mine.reshape(1, windows * quarter, span)
    if chans == 8 and span == CHUNK:
        pair = jnp.concatenate([held, swap(held, "chan", 1)], axis=0)
        pair, prepared = lax.optimization_barrier((pair, prepared))
        flips = (6, 4, 2)
        parts = [pair] + [swap(pair, "chan", flip) for flip in flips]
        return prepared, parts, tuple((flip, flip ^ 1) for flip in (0,) + flips)
    keys, flip = [0], 1
    while flip < chans:
        held = jnp.concatenate([held, swap(held, "chan", flip)], axis=0)
        keys = keys + [key ^ flip for key in keys]
        flip *= 2
    every = jnp.zeros_like(held).at[chan ^ jnp.asarray(keys, jnp.int32)].set(held)
    every = regroup(every)
    return prepared, (every,), ((None,) * every.shape[0],)


def shards(records, sources, dead_list):
    windows, groups, width, span = records.shape
    reps, chans = lax.axis_size("rep"), lax.axis_size("chan")
    cw = width * reps
    per = groups // chans
    blocks, *low, high = pack(records, sources, chans, reps)
    blocks = blocks.reshape(chans, windows * per * width, span)
    order = order_of(chans)
    arrived = lax.all_to_all(blocks, "chan", 0, 0, axis_index_groups=[list(order)], tiled=True)
    if span != CHUNK:
        arrived = regroup(jnp.stack([arrived[order.index(i)] for i in range(chans)]))
        order = tuple(range(arrived.shape[0]))
    table = jnp.asarray(dft_table(chans * span))

    def prepare(after):
        return stage(table, sources, dead_list, after, per, cw, width)

    (table, live, source_live, scale), parts, keys = gather_sources(low, high, prepare)
    tables = [table, jnp.asarray(sample_band()), jnp.asarray(bin_band())]
    spectra = channel_spectra(arrived, order, live, tables, windows)
    source_spec = source_spectra(parts, keys, source_live, tables)
    pieces, flips = [spectra], [0]
    flip = reps // 2
    while flip:
        others = [swap(piece, "rep", flip) for piece in pieces]
        pieces = pieces + others
        flips = flips + [f ^ flip for f in flips]
        flip //= 2
    left = lag_kernels(source_spec, windows)
    return correlate(pieces, flips, left, scale, cw)


def solution(mesh):
    placed = (P(None, None, "rep", "chan"), P(), P())
    return jax.shard_map(
        shards, mesh=mesh, in_specs=placed, out_specs=P("rep", None, "chan"), check_vma=False
    )
```

```python
import functools
import math

import jax
import jax.numpy as jnp
import numpy as np
from jax import lax
from jax.experimental import pallas as pl
from jax.experimental.pallas import tpu as pltpu
from jax.sharding import PartitionSpec as P

WINDOW_SAMPLES = 2048
K = 256
K0 = 16
HALF = 32
WH = 32
LAGS = 64
EPS = 1e-06

CHUNK = 256
EDGE = 128
ORDER = (3, 6, 1, 2, 7, 0, 5, 4)
VMEM = pl.BlockSpec(memory_space=pltpu.VMEM)
LIMIT = 16 * 1024 * 1024
STAGE_FLOPS = 1
HBM = pl.BlockSpec(memory_space=pltpu.HBM)


def dft_table(length):
    sample = np.arange(length, dtype=np.int64)[:, None]
    bin_index = K0 + np.arange(K, dtype=np.int64)[None, :]
    angle = (sample * bin_index % length) * (2.0 * math.pi / length)
    table = np.concatenate([np.cos(angle), -np.sin(angle)], axis=1)
    return table.astype(np.float32).astype(jnp.bfloat16)


def lag_tables():
    bin_index = K0 + np.arange(K, dtype=np.int64)[None, :]
    lag = np.arange(LAGS, dtype=np.int64)[:, None] - LAGS // 2
    angle = np.mod(lag * bin_index, WINDOW_SAMPLES) * (2.0 * math.pi / WINDOW_SAMPLES)
    return np.cos(angle).astype(np.float32), np.sin(angle).astype(np.float32)


def sample_band():
    source = np.arange(CHUNK + 2 * EDGE)[:, None] - EDGE
    target = np.arange(CHUNK)[None, :]
    return (np.abs(source - target) <= HALF).astype(np.float32).astype(jnp.bfloat16)


def bin_band():
    row = np.arange(K)[:, None]
    column = np.arange(K)[None, :]
    return (np.abs(row - column) <= WH).astype(np.float32).astype(jnp.bfloat16)


def order_of(chans):
    return ORDER if chans == len(ORDER) else tuple(range(chans))


def iota(shape, dim):
    return lax.broadcasted_iota(jnp.int32, shape, dim)


def columns_of(row):
    return jnp.concatenate(
        [
            jnp.broadcast_to(row[:, i : i + 128], (128, 128)).T
            for i in range(0, row.shape[1], 128)
        ],
        axis=0,
    )


def listed(ids, dead):
    hit = jnp.zeros((ids.shape[0], 128), jnp.float32)
    for i in range(0, dead.shape[1], 128):
        hit = jnp.maximum(hit, jnp.where(ids == dead[:, i : i + 128], 1.0, 0.0))
    return jnp.max(hit, axis=1, keepdims=True)


def pack_kernel(cw, rec_hbm, src_hbm, out_hbm, *refs):
    *low_refs, high_ref, out_ref, src_ref, pick_ref, sem = refs
    windows, groups, width, span = rec_hbm.shape
    per = groups // out_ref.shape[0]
    order = order_of(out_ref.shape[0])
    brought = pltpu.make_async_copy(src_hbm, src_ref, sem.at[windows, 0])
    brought.start()
    copies = []
    for w in range(windows):
        copies.append(
            [
                pltpu.make_async_copy(
                    rec_hbm.at[w, pl.ds(member * per, per)], out_ref.at[n, w], sem.at[w, n]
                )
                for n, member in enumerate(order)
            ]
        )
        for copy in copies[-1]:
            copy.start()
    reps = cw // width
    rep = lax.axis_index("rep")
    count = src_ref.shape[1]
    quarter = count // reps
    local = groups * width
    place = iota((count, local), 1)
    ids = (place // width) * cw + rep * width + place % width
    brought.wait()
    wide = jnp.concatenate([columns_of(src_ref[...])] * (local // 128), axis=1)
    onehot = jnp.where(wide == ids, 1.0, 0.0).astype(jnp.bfloat16)
    sent = []
    for w in range(windows):
        for n in range(len(order)):
            copies[w][n].wait()
            sent.append(
                pltpu.make_async_copy(out_ref.at[n, w], out_hbm.at[n, w], sem.at[windows + 1 + w, n])
            )
            sent[-1].start()
    for w in range(windows):
        rows = jnp.concatenate(
            [out_ref[order.index(g // per), w, g % per] for g in range(groups)], axis=0
        )
        pick_ref[...] = jnp.dot(onehot, rows, preferred_element_type=jnp.float32)
        for flip in range(reps):
            first = pl.multiple_of((rep ^ flip) * quarter, quarter)
            picked = pick_ref[pl.ds(first, quarter), :].astype(jnp.bfloat16)
            if flip < reps // 2:
                low_refs[flip][w] = picked
            else:
                high_ref[flip - reps // 2, w] = picked
    for copy in sent:
        copy.wait()


def in_hbm(*arrays):
    return [pltpu.with_memory_space_constraint(array, pltpu.HBM) for array in arrays]


def pack(records, sources, chans, reps):
    windows, groups, width, span = records.shape
    count = sources.shape[0]
    per = groups // chans
    part = (windows, count // reps, span)
    return pl.pallas_call(
        functools.partial(pack_kernel, width * reps),
        out_shape=(
            jax.ShapeDtypeStruct((chans, windows, per, width, span), jnp.bfloat16),
            *[jax.ShapeDtypeStruct(part, jnp.bfloat16)] * (reps // 2),
            jax.ShapeDtypeStruct((reps // 2,) + part, jnp.bfloat16),
        ),
        in_specs=[HBM] * 2,
        out_specs=(HBM,) + (VMEM,) * (reps // 2 + 1),
        scratch_shapes=[
            pltpu.VMEM((chans, windows, per, width, span), jnp.bfloat16),
            pltpu.VMEM((1, count), jnp.int32),
            pltpu.VMEM((count, span), jnp.float32),
            pltpu.SemaphoreType.DMA((1 + 2 * windows, chans)),
        ],
        compiler_params=pltpu.CompilerParams(vmem_limit_bytes=LIMIT),
        name="pack",
    )(*in_hbm(records, sources.reshape(1, count)))


def stage_kernel(
    cw, width, table_hbm, src_hbm, dead_hbm, after_hbm,
    table_ref, live_ref, source_live_ref, scale_ref,
    src_ref, dead_ref, pick_ref, sem,
):
    copies = [
        pltpu.make_async_copy(src_hbm, src_ref, sem.at[0]),
        pltpu.make_async_copy(dead_hbm, dead_ref, sem.at[1]),
        pltpu.make_async_copy(table_hbm, table_ref, sem.at[2]),
    ]
    for copy in copies:
        copy.start()
    windows = dead_ref.shape[0]
    rep, chan = lax.axis_index("rep"), lax.axis_index("chan")
    count = src_ref.shape[1]
    quarter, columns = scale_ref.shape
    per = columns // cw
    here = pl.ds(pl.multiple_of(rep * quarter, quarter), quarter)
    row = iota((per * width, 1), 0)
    row_ids = (chan * per + row // width) * cw + rep * width + row % width
    block_ids = chan * columns + iota((1, columns), 1)
    copies[0].wait()
    copies[1].wait()
    column = columns_of(src_ref[...])
    pick_ref[...] = column
    mine = pick_ref[here, :]
    pairs = jnp.zeros((quarter, columns), jnp.float32)
    for w in range(windows):
        dead = dead_ref[w : w + 1, :]
        live_ref[w * per * width : (w + 1) * per * width, :] = 1.0 - listed(row_ids, dead)
        source_live = 1.0 - listed(mine, dead)
        source_live_ref[w * quarter : (w + 1) * quarter, :] = source_live
        dead_column = columns_of(dead)
        hits = [
            jnp.max(
                jnp.where(dead_column == block_ids[:, i : i + 128], 1.0, 0.0), axis=0, keepdims=True
            )
            for i in range(0, columns, 128)
        ]
        pairs += source_live * (1.0 - jnp.concatenate(hits, axis=1))
    scale_ref[...] = 1.0 / (math.sqrt(K) * jnp.maximum(pairs, 1.0))
    copies[2].wait()


def stage(table, sources, dead_list, after, per, cw, width):
    windows = dead_list.shape[0]
    count = sources.shape[0]
    quarter = count // (cw // width)
    return pl.pallas_call(
        functools.partial(stage_kernel, cw, width),
        out_shape=(
            jax.ShapeDtypeStruct(table.shape, table.dtype),
            jax.ShapeDtypeStruct((windows * per * width, 1), jnp.float32),
            jax.ShapeDtypeStruct((windows * quarter, 1), jnp.float32),
            jax.ShapeDtypeStruct((quarter, per * cw), jnp.float32),
        ),
        in_specs=[HBM] * 3 + [pl.BlockSpec(memory_space=pl.ANY)],
        out_specs=(VMEM,) * 4,
        scratch_shapes=[
            pltpu.VMEM((1, count), jnp.int32),
            pltpu.VMEM(dead_list.shape, jnp.int32),
            pltpu.VMEM((count, 128), jnp.int32),
            pltpu.SemaphoreType.DMA((3,)),
        ],
        compiler_params=pltpu.CompilerParams(vmem_limit_bytes=LIMIT),
        cost_estimate=pl.CostEstimate(
            flops=STAGE_FLOPS, bytes_accessed=4 << 20, transcendentals=0
        ),
        name="stage",
    )(*in_hbm(table, sources.reshape(1, count), dead_list), after)


def whiten_rows(x_ref, order, group, table_ref, band_ref, bins_ref):
    pieces, rows, _ = x_ref.shape
    x = [x_ref.at[order.index(i)] for i in range(pieces)]
    length = pieces * CHUNK
    views, chunks = [], []
    blank = jnp.zeros((rows, EDGE), jnp.bfloat16)
    for i in range(pieces):
        before = jnp.abs(x[i - 1][:, CHUNK - EDGE :]) if i else blank
        after = jnp.abs(x[i + 1][:, :EDGE]) if i < pieces - 1 else blank
        views.append(jnp.concatenate([before, jnp.abs(x[i][...]), after], axis=1))
    for i in range(pieces):
        n = i % group
        if n == 0:
            view = jnp.concatenate(views[i : i + group], axis=0)
            totals = jnp.dot(view, band_ref[...], preferred_element_type=jnp.float32)
        sample = iota((1, CHUNK), 1) + i * CHUNK
        counts = jnp.minimum(sample, HALF) + jnp.minimum(length - 1 - sample, HALF) + 1
        mean = totals[n * rows : (n + 1) * rows] * (1.0 / counts.astype(jnp.float32))
        chunks.append((x[i][...].astype(jnp.float32) / (mean + EPS)).astype(jnp.bfloat16))
    spectrum = jnp.dot(
        jnp.concatenate(chunks, axis=1), table_ref[...], preferred_element_type=jnp.float32
    )
    real_part, imag_part = spectrum[:, :K], spectrum[:, K:]
    amplitude = jnp.sqrt(real_part * real_part + imag_part * imag_part)
    high = amplitude.astype(jnp.bfloat16)
    rest = amplitude - high.astype(jnp.float32)
    middle = rest.astype(jnp.bfloat16)
    low = (rest - middle.astype(jnp.float32)).astype(jnp.bfloat16)
    stacked = jnp.concatenate([high, middle, low], axis=0)
    sums = jnp.dot(stacked, bins_ref[...], preferred_element_type=jnp.float32)
    place = iota((1, K), 1)
    width = jnp.minimum(place, WH) + jnp.minimum(K - 1 - place, WH) + 1
    smooth = (sums[:rows] + sums[rows : 2 * rows] + sums[2 * rows :]) * (
        1.0 / width.astype(jnp.float32)
    )
    scale = 1.0 / (smooth + EPS)
    return real_part * scale, imag_part * scale


def channel_kernel(order, x_ref, live_ref, table_ref, band_ref, bins_ref, out_ref):
    windows, count, _ = out_ref.shape
    real_part, imag_part = whiten_rows(x_ref, order, 2, table_ref, band_ref, bins_ref)
    for w in range(windows):
        here = slice(w * count, (w + 1) * count)
        out_ref[w, :, :K] = (real_part[here] * live_ref[here, :]).astype(jnp.bfloat16)
        out_ref[w, :, K:] = (imag_part[here] * live_ref[here, :]).astype(jnp.bfloat16)


def channel_spectra(x, order, live, tables, windows):
    pieces, rows, _ = x.shape
    return pl.pallas_call(
        functools.partial(channel_kernel, order),
        out_shape=jax.ShapeDtypeStruct((windows, rows // windows, 2 * K), jnp.bfloat16),
        in_specs=[VMEM] * 5,
        out_specs=VMEM,
        compiler_params=pltpu.CompilerParams(vmem_limit_bytes=LIMIT),
        cost_estimate=pl.CostEstimate(
            flops=1, bytes_accessed=1, transcendentals=0
        ),
        name="channel_spectra",
    )(x, live, *tables)


def source_kernel(keys, *refs):
    parts = refs[: len(keys)]
    live_ref, table_ref, band_ref, bins_ref = refs[len(keys) : -2]
    out_ref, x_ref = refs[-2:]
    chan = lax.axis_index("chan")
    for part, slots in zip(parts, keys):
        for n, key in enumerate(slots):
            x_ref[chan ^ key if key is not None else n] = part[n]
    order = tuple(range(x_ref.shape[0]))
    real_part, imag_part = whiten_rows(x_ref, order, len(order), table_ref, band_ref, bins_ref)
    out_ref[:, :K] = (real_part * live_ref[...]).astype(jnp.bfloat16)
    out_ref[:, K:] = (imag_part * live_ref[...]).astype(jnp.bfloat16)


def source_spectra(parts, keys, live, tables):
    rows = parts[0].shape[1]
    pieces = sum(len(slots) for slots in keys)
    return pl.pallas_call(
        functools.partial(source_kernel, keys),
        out_shape=jax.ShapeDtypeStruct((rows, 2 * K), jnp.bfloat16),
        in_specs=[VMEM] * (len(parts) + 4),
        out_specs=VMEM,
        scratch_shapes=[
            pltpu.VMEM((pieces, rows, CHUNK), jnp.bfloat16),
        ],
        compiler_params=pltpu.CompilerParams(vmem_limit_bytes=LIMIT),
        cost_estimate=pl.CostEstimate(flops=1 << 34, bytes_accessed=8 << 20, transcendentals=0),
        name="source_spectra",
    )(*parts, live, *tables)


def lag_kernel(windows, spec_ref, cos_ref, sin_ref, out_ref):
    spec = spec_ref[...].astype(jnp.float32)
    quarter = spec.shape[0] // windows
    lags = cos_ref.shape[0]
    for s in range(quarter):
        for w in range(windows):
            u = spec[w * quarter + s : w * quarter + s + 1, :K]
            v = spec[w * quarter + s : w * quarter + s + 1, K:]
            rows = slice(s * lags, (s + 1) * lags)
            first = w * 2 * K
            out_ref[rows, first : first + K] = (
                u * cos_ref[...] + v * sin_ref[...]
            ).astype(jnp.bfloat16)
            out_ref[rows, first + K : first + 2 * K] = (
                v * cos_ref[...] - u * sin_ref[...]
            ).astype(jnp.bfloat16)


def lag_kernels(spec, windows):
    rows = spec.shape[0]
    cosine, sine = lag_tables()
    return pl.pallas_call(
        functools.partial(lag_kernel, windows),
        out_shape=jax.ShapeDtypeStruct((rows // windows * LAGS, windows * 2 * K), jnp.bfloat16),
        in_specs=[VMEM] * 3,
        out_specs=VMEM,
        compiler_params=pltpu.CompilerParams(vmem_limit_bytes=LIMIT),
        cost_estimate=pl.CostEstimate(flops=1 << 34, bytes_accessed=8 << 20, transcendentals=0),
        name="lag_kernels",
    )(spec, jnp.asarray(cosine), jnp.asarray(sine))


def correlate_kernel(flips, cw, *refs):
    parts = refs[: len(flips)]
    left_ref, scale_ref, out_hbm, right_ref, out_ref, sem = refs[len(flips) :]
    windows, count, features = parts[0].shape
    steps, batch, lags, columns = out_ref.shape
    per = columns // cw
    width = count // per
    rep = lax.axis_index("rep")
    for part, flip in zip(parts, flips):
        for w in range(windows):
            for g in range(per):
                first = pl.multiple_of(g * cw + (rep ^ flip) * width, width)
                right_ref[pl.ds(first, width), pl.ds(w * features, features)] = part[
                    w, pl.ds(g * width, width), :
                ]
    copies = []
    for i in range(steps):
        summed = lax.dot_general(
            left_ref[i * batch * lags : (i + 1) * batch * lags, :],
            right_ref[...],
            (((1,), (1,)), ((), ())),
            preferred_element_type=jnp.float32,
        )
        for n in range(batch):
            s = i * batch + n
            out_ref[i, n] = summed[n * lags : (n + 1) * lags] * scale_ref[s : s + 1, :]
        copies.append(
            pltpu.make_async_copy(
                out_ref.at[i], out_hbm.at[pl.ds(i * batch, batch)], sem.at[i]
            )
        )
        copies[-1].start()
    for copy in copies:
        copy.wait()


def correlate(parts, flips, left, scale, cw):
    quarter, columns = scale.shape
    steps = 8
    return pl.pallas_call(
        functools.partial(correlate_kernel, flips, cw),
        out_shape=jax.ShapeDtypeStruct((quarter, LAGS, columns), jnp.float32),
        in_specs=[VMEM] * (len(parts) + 2),
        out_specs=HBM,
        scratch_shapes=[
            pltpu.VMEM((columns, left.shape[1]), jnp.bfloat16),
            pltpu.VMEM((steps, quarter // steps, LAGS, columns), jnp.float32),
            pltpu.SemaphoreType.DMA((steps,)),
        ],
        compiler_params=pltpu.CompilerParams(vmem_limit_bytes=LIMIT),
        name="correlate",
    )(*parts, left, scale)


def swap(x, axis, flip):
    size = lax.axis_size(axis)
    return lax.ppermute(x, axis, [(i, i ^ flip) for i in range(size)])


def regroup(x):
    shards_in, rows, span = x.shape
    if span == CHUNK:
        return x
    joined = jnp.transpose(x, (1, 0, 2)).reshape(rows, -1, CHUNK)
    return jnp.transpose(joined, (1, 0, 2))


def gather_sources(low, high, prepare):
    chans, chan = lax.axis_size("chan"), lax.axis_index("chan")
    windows, quarter, span = low[0].shape
    given = list(low) + [high[n] for n in range(len(low))]
    mine = given[0]
    for flip in range(1, len(given)):
        mine = mine + swap(given[flip], "rep", flip)
    prepared = prepare(mine)
    held = mine.reshape(1, windows * quarter, span)
    if chans == 8 and span == CHUNK:
        pair = jnp.concatenate([held, swap(held, "chan", 1)], axis=0)
        pair, prepared = lax.optimization_barrier((pair, prepared))
        flips = (6, 4, 2)
        parts = [pair] + [swap(pair, "chan", flip) for flip in flips]
        return prepared, parts, tuple((flip, flip ^ 1) for flip in (0,) + flips)
    keys, flip = [0], 1
    while flip < chans:
        held = jnp.concatenate([held, swap(held, "chan", flip)], axis=0)
        keys = keys + [key ^ flip for key in keys]
        flip *= 2
    every = jnp.zeros_like(held).at[chan ^ jnp.asarray(keys, jnp.int32)].set(held)
    every = regroup(every)
    return prepared, (every,), ((None,) * every.shape[0],)


def shards(records, sources, dead_list):
    windows, groups, width, span = records.shape
    reps, chans = lax.axis_size("rep"), lax.axis_size("chan")
    cw = width * reps
    per = groups // chans
    blocks, *low, high = pack(records, sources, chans, reps)
    blocks = blocks.reshape(chans, windows * per * width, span)
    order = order_of(chans)
    arrived = lax.all_to_all(blocks, "chan", 0, 0, axis_index_groups=[list(order)], tiled=True)
    if span != CHUNK:
        arrived = regroup(jnp.stack([arrived[order.index(i)] for i in range(chans)]))
        order = tuple(range(arrived.shape[0]))
    table = jnp.asarray(dft_table(chans * span))

    def prepare(after):
        return stage(table, sources, dead_list, after, per, cw, width)

    (table, live, source_live, scale), parts, keys = gather_sources(low, high, prepare)
    tables = [table, jnp.asarray(sample_band()), jnp.asarray(bin_band())]
    spectra = channel_spectra(arrived, order, live, tables, windows)
    source_spec = source_spectra(parts, keys, source_live, tables)
    pieces, flips = [spectra], [0]
    flip = reps // 2
    while flip:
        others = [swap(piece, "rep", flip) for piece in pieces]
        pieces = pieces + others
        flips = flips + [f ^ flip for f in flips]
        flip //= 2
    left = lag_kernels(source_spec, windows)
    return correlate(pieces, flips, left, scale, cw)


def solution(mesh):
    placed = (P(None, None, "rep", "chan"), P(), P())
    return jax.shard_map(
        shards, mesh=mesh, in_specs=placed, out_specs=P("rep", None, "chan"), check_vma=False
    )
```
